32 devices in a mesh: ctx: 16 (over z, y, x), dp: 2 (over core).
Axes of the slice: x: 2, y: 2, z: 4, core: 2. Of those that a mesh axis runs over, the one named last changes fastest.
Arguments:
- att_query: bfloat16 [4096, 4096], P(('dp', 'ctx')), parts along dimension 0, may hold values from -126 to 126
- att_key: bfloat16 [4096, 4096], P(('dp', 'ctx')), parts along dimension 0, may hold values from -6 to 6
- att_value: bfloat16 [4096, 4096], P(('dp', 'ctx')), parts along dimension 0, may hold values from -6 to 6
Outputs:
- attn_out: bfloat16 [4096, 4096], P(('dp', 'ctx')), parts along dimension 0
- attn_lse: float32 [32, 4096], P(None, ('dp', 'ctx')), parts along dimension 1
The draws below stay inside these ranges and needn't reach their ends.
There are 2 independent parts, one for each index of `dp`. The reference program is written for one: setup_inputs(seed, part) draws one part's arguments, and reference() takes and returns one part's arrays. A program takes and returns all parts, laid end to end along the dimension named above; each array names one. Nothing has to cross between parts.
All inputs are finite; a program needn't handle non-finite values.
Results may differ from the reference program's by a relative error of at most 0.0045.
Values may be sent and summed in bfloat16 or wider, within the bound.
A program may use at most 64 MiB of HBM per device.

```python
import math
import jax
import jax.numpy as jnp
from jax import lax

HEADS = 32
HEAD_DIM = 128
KV_STEPS = 3
TOK_DEV = 128
SEQ = 2048
N_CTX = 16


def attention_pair(key):
    att_width = HEADS * HEAD_DIM
    key_base = jnp.clip(jax.random.normal(jax.random.fold_in(key, 71), (SEQ, att_width), jnp.float32), -6.0, 6.0)
    query_base = jnp.clip(jax.random.normal(jax.random.fold_in(key, 72), (SEQ, att_width), jnp.float32), -6.0, 6.0)
    return (query_base, key_base)


def draw_att_query(key, part):
    return attention_pair(key)[0].astype(jnp.bfloat16)


def draw_att_key(key, part):
    return attention_pair(key)[1].astype(jnp.bfloat16)


def level_of(stream_key, dims, shards, smallest, largest):
    factor_of = 1.0
    for dim, shards_of in shards:
        heights = jax.random.uniform(jax.random.fold_in(jax.random.fold_in(stream_key, 6), dim), (shards_of,), jnp.float32, smallest / len(shards), largest / len(shards))
        factor_of = factor_of * jnp.repeat(jnp.exp(heights), dims[dim] // shards_of).reshape((-1,) + (1,) * (len(dims) - 1 - dim))
    return factor_of


def centred(rng, dims, width, reach, shards=(), kind=jnp.bfloat16):
    drawn = width * jax.random.normal(rng, dims, jnp.float32)
    if shards:
        drawn = drawn * level_of(rng, dims, shards, -0.22, 0.18)
    return jnp.clip(drawn, -reach, reach).astype(kind)


def setup_inputs(seed: int = 0, part: int = 0) -> dict:
    keys = jax.random.split(jax.random.key(seed), 4)
    part_splits = jax.random.split(jax.random.fold_in(keys[3], part), 4)
    return {
        "att_query": draw_att_query(jax.random.fold_in(jax.random.fold_in(keys[3], part), 71), part),
        "att_key": draw_att_key(jax.random.fold_in(jax.random.fold_in(keys[3], part), 71), part),
        "att_value": centred(part_splits[2], (SEQ, HEADS * HEAD_DIM), 1.0, 6.0, ((0, 16),)),
    }


def attend(query_rows, key_rows, value_rows, key_start, query_start):
    row_count = query_rows.shape[0]
    key_count = key_rows.shape[0]
    head_count = query_rows.shape[1] // HEAD_DIM
    queries = query_rows.astype(jnp.float32).reshape(row_count, head_count, HEAD_DIM)
    key_heads = key_rows.astype(jnp.float32).reshape(key_count, head_count, HEAD_DIM)
    value_heads = value_rows.astype(jnp.float32).reshape(key_count, head_count, HEAD_DIM)
    scores = jnp.einsum('thd,shd->hts', queries, key_heads, precision=lax.Precision.HIGHEST) * (1.0 / math.sqrt(HEAD_DIM))
    key_place = key_start + jnp.arange(key_count, dtype=jnp.int32)
    query_place = query_start + jnp.arange(row_count, dtype=jnp.int32)
    allowed = (key_place[None, :] >= 0) & (key_place[None, :] <= query_place[:, None])
    scores = jnp.where(allowed[None], scores, -jnp.inf)
    row_max = lax.optimization_barrier(jnp.max(scores, axis=2, keepdims=True))
    weights = jnp.exp(scores - row_max)
    denominator = lax.optimization_barrier(jnp.sum(weights, axis=2))
    rounded = lax.optimization_barrier(weights.astype(jnp.bfloat16)).astype(jnp.float32)
    mixed = jnp.einsum('hts,shd->thd', rounded, value_heads, precision=lax.Precision.HIGHEST)
    output = (mixed / jnp.transpose(denominator)[:, :, None]).reshape(row_count, head_count * HEAD_DIM).astype(jnp.bfloat16)
    return (output, row_max[:, :, 0] + jnp.log(denominator))

def reference(att_query, att_key, att_value):
    lead_rows = (KV_STEPS - 1) * TOK_DEV
    att_width = att_key.shape[1]
    key_padded = jnp.concatenate([jnp.zeros((lead_rows, att_width), att_key.dtype), att_key], axis=0)
    value_padded = jnp.concatenate([jnp.zeros((lead_rows, att_width), att_value.dtype), att_value], axis=0)

    def attention_block(block_index):
        query_rows = lax.dynamic_slice_in_dim(att_query, block_index * TOK_DEV, TOK_DEV, 0)
        key_rows = lax.dynamic_slice_in_dim(key_padded, block_index * TOK_DEV, KV_STEPS * TOK_DEV, 0)
        value_rows = lax.dynamic_slice_in_dim(value_padded, block_index * TOK_DEV, KV_STEPS * TOK_DEV, 0)
        return attend(query_rows, key_rows, value_rows, (block_index - (KV_STEPS - 1)) * TOK_DEV, block_index * TOK_DEV)
    mixed, log_total = lax.map(attention_block, jnp.arange(N_CTX, dtype=jnp.int32))
    attn_out = mixed.reshape(SEQ, att_width)
    attn_lse = jnp.moveaxis(log_total, 0, 1).reshape(log_total.shape[1], SEQ)
    return (attn_out, attn_lse)
```

```python
import functools
import math

import jax
import jax.numpy as jnp
from jax import lax
from jax.experimental import pallas as pl
from jax.experimental.pallas import tpu as pltpu
from jax.sharding import PartitionSpec as P

HEAD_DIM = 128
KV_STEPS = 3
CHUNK_HEADS = 2
AHEAD_ODD = 4
MESH = pl.DeviceIdType.MESH


def kernel(
    n, q_hbm, k_hbm, v_hbm, o_ref, lse_ref,
    q_buf, k_buf, v_buf, bias,
    in_sem, far_send, far_recv, near_send, near_recv,
):
    chunks, rows, width = q_buf.shape
    me = lax.axis_index("ctx")
    odd = lax.rem(me, 2)
    even = odd == 0
    partner = me + 1 - 2 * odd
    has_far_target = me + 2 < n
    has_far_source = me >= 2
    has_near_source = me >= 1
    hbm = (k_hbm, v_hbm)
    bufs = (k_buf, v_buf)

    def columns(c):
        return pl.ds(pl.multiple_of(c * width, width), width)

    def far(c, t):
        return pltpu.make_async_remote_copy(
            src_ref=hbm[t].at[:, columns(c)], dst_ref=bufs[t].at[c, 2],
            send_sem=far_send.at[c, t], recv_sem=far_recv.at[c, t],
            device_id={"ctx": lax.rem(me + 2, n)}, device_id_type=MESH)

    def near(c, t):
        return pltpu.make_async_remote_copy(
            src_ref=hbm[t].at[:, columns(c)], dst_ref=bufs[t].at[c, 1],
            send_sem=near_send.at[c, t], recv_sem=near_recv.at[c, t],
            device_id={"ctx": partner}, device_id_type=MESH)

    def relay(c, t):
        return pltpu.make_async_remote_copy(
            src_ref=bufs[t].at[c, 2], dst_ref=bufs[t].at[c, 1],
            send_sem=near_send.at[c, t], recv_sem=near_recv.at[c, t],
            device_id={"ctx": partner}, device_id_type=MESH)

    def local(c):
        return [
            pltpu.make_async_copy(q_hbm.at[:, columns(c)], q_buf.at[c], in_sem.at[c, 0]),
            pltpu.make_async_copy(k_hbm.at[:, columns(c)], k_buf.at[c, 0], in_sem.at[c, 1]),
            pltpu.make_async_copy(v_hbm.at[:, columns(c)], v_buf.at[c, 0], in_sem.at[c, 2]),
        ]

    barrier = pltpu.get_barrier_semaphore()
    pl.semaphore_signal(barrier, inc=1, device_id={"ctx": partner}, device_id_type=MESH)

    @pl.when(has_far_target)
    def _():
        pl.semaphore_signal(barrier, inc=1, device_id={"ctx": lax.rem(me + 2, n)}, device_id_type=MESH)

    @pl.when(has_far_source)
    def _():
        pl.semaphore_signal(barrier, inc=1, device_id={"ctx": lax.rem(me + n - 2, n)}, device_id_type=MESH)

    def start_local(c, carry):
        for copy in local(c):
            copy.start()
        return carry

    lax.fori_loop(0, chunks, start_local, 0)

    pl.semaphore_wait(barrier, 1 + has_far_target.astype(jnp.int32) + has_far_source.astype(jnp.int32))

    def start_far(c):
        @pl.when(has_far_target)
        def _():
            for t in range(2):
                far(c, t).start()

    @pl.when(even)
    def _():
        def start_own(c, carry):
            for t in range(2):
                near(c, t).start()
            start_far(c)
            return carry
        lax.fori_loop(0, chunks, start_own, 0)

    @pl.when(odd == 1)
    def _():
        def start_own(c, carry):
            start_far(c)
            return carry
        lax.fori_loop(0, AHEAD_ODD, start_own, 0)

    query = lax.broadcasted_iota(jnp.int32, (rows, KV_STEPS * rows), 0)
    key = lax.broadcasted_iota(jnp.int32, (rows, KV_STEPS * rows), 1)
    slot = key // rows
    allowed = (slot <= me) & ((slot > 0) | (key <= query))
    bias[...] = jnp.where(allowed, 0.0, -jnp.inf)
    factor = math.log2(math.e) / math.sqrt(HEAD_DIM)

    def step(c, carry):
        for copy in local(c):
            copy.wait()

        @pl.when(has_far_source)
        def _():
            for t in range(2):
                far(c, t).wait_recv()

            @pl.when(odd == 1)
            def _():
                for t in range(2):
                    relay(c, t).start()

        @pl.when((odd == 1) & (c + AHEAD_ODD < chunks))
        def _():
            start_far(c + AHEAD_ODD)

        @pl.when(has_near_source)
        def _():
            for t in range(2):
                near(c, t).wait_recv()

        @pl.when(jnp.logical_not(has_far_source))
        def _():
            k_buf[c, 2] = jnp.zeros((rows, width), jnp.bfloat16)
            v_buf[c, 2] = jnp.zeros((rows, width), jnp.bfloat16)

        @pl.when(jnp.logical_not(has_near_source))
        def _():
            k_buf[c, 1] = jnp.zeros((rows, width), jnp.bfloat16)
            v_buf[c, 1] = jnp.zeros((rows, width), jnp.bfloat16)

        for h in range(width // HEAD_DIM):
            cols = slice(h * HEAD_DIM, (h + 1) * HEAD_DIM)
            q = q_buf[c, :, cols]
            k = k_buf[c, :, :, cols].reshape(KV_STEPS * rows, HEAD_DIM)
            v = v_buf[c, :, :, cols].reshape(KV_STEPS * rows, HEAD_DIM)
            s = lax.dot_general(q, k, (((1,), (1,)), ((), ())), preferred_element_type=jnp.float32)
            s = s + bias[...]
            m = jnp.max(s, axis=1, keepdims=True)
            w = jnp.exp2((s - m) * factor)
            total = jnp.sum(w, axis=1, keepdims=True)
            mixed = jnp.dot(w.astype(jnp.bfloat16), v, preferred_element_type=jnp.float32)
            place = pl.ds(pl.multiple_of(c * width + h * HEAD_DIM, HEAD_DIM), HEAD_DIM)
            o_ref[:, place] = (mixed / total).astype(o_ref.dtype)
            lse = m * (1.0 / math.sqrt(HEAD_DIM)) + jnp.log(total)
            diagonal = (lax.broadcasted_iota(jnp.int32, (rows, rows), 0)
                        == lax.broadcasted_iota(jnp.int32, (rows, rows), 1))
            lse_ref[pl.ds(c * (width // HEAD_DIM) + h, 1), :] = jnp.sum(
                jnp.where(diagonal, lse, 0.0), axis=0, keepdims=True)
        return carry

    lax.fori_loop(0, chunks, step, 0)

    def finish(c, carry):
        @pl.when(has_far_target)
        def _():
            for t in range(2):
                far(c, t).wait_send()

        @pl.when(even | has_far_source)
        def _():
            for t in range(2):
                near(c, t).wait_send()
        return carry

    lax.fori_loop(0, chunks, finish, 0)


def shards(n, att_query, att_key, att_value):
    rows, total_width = att_query.shape
    heads = total_width // HEAD_DIM
    chunk_heads = math.gcd(heads, CHUNK_HEADS)
    chunks, width = heads // chunk_heads, chunk_heads * HEAD_DIM
    bf16 = att_query.dtype
    return pl.pallas_call(
        functools.partial(kernel, n),
        out_shape=(
            jax.ShapeDtypeStruct((rows, total_width), bf16),
            jax.ShapeDtypeStruct((heads, rows), jnp.float32),
        ),
        in_specs=[pl.BlockSpec(memory_space=pltpu.HBM)] * 3,
        out_specs=(pl.BlockSpec(memory_space=pltpu.VMEM), pl.BlockSpec(memory_space=pltpu.VMEM)),
        scratch_shapes=[
            pltpu.VMEM((chunks, rows, width), bf16),
            pltpu.VMEM((chunks, KV_STEPS, rows, width), bf16),
            pltpu.VMEM((chunks, KV_STEPS, rows, width), bf16),
            pltpu.VMEM((rows, KV_STEPS * rows), jnp.float32),
            pltpu.SemaphoreType.DMA((chunks, 3)),
            pltpu.SemaphoreType.DMA((chunks, 2)),
            pltpu.SemaphoreType.DMA((chunks, 2)),
            pltpu.SemaphoreType.DMA((chunks, 2)),
            pltpu.SemaphoreType.DMA((chunks, 2)),
        ],
        compiler_params=pltpu.CompilerParams(
            collective_id=0, has_side_effects=True, vmem_limit_bytes=60 * 1024 * 1024),
        cost_estimate=pl.CostEstimate(
            flops=4 * rows * rows * KV_STEPS * total_width,
            bytes_accessed=8 * rows * total_width,
            transcendentals=rows * rows * KV_STEPS * heads),
    )(att_query, att_key, att_value)


def solution(mesh):
    spec = P(("dp", "ctx"), None)
    return jax.shard_map(
        functools.partial(shards, mesh.shape["ctx"]),
        mesh=mesh,
        in_specs=(spec, spec, spec),
        out_specs=(spec, P(None, ("dp", "ctx"))),
        check_vma=False,
    )
```

```python
import functools
import math

import jax
import jax.numpy as jnp
from jax import lax
from jax.experimental import pallas as pl
from jax.experimental.pallas import tpu as pltpu
from jax.sharding import PartitionSpec as P

HEAD_DIM = 128
KV_STEPS = 3
CHUNK_HEADS = 4
AHEAD_ODD = 3
MESH = pl.DeviceIdType.MESH


def kernel(
    n, q_hbm, k_hbm, v_hbm, o_ref, lse_ref,
    q_own, k_own, v_own, k_buf, v_buf, bias,
    in_sem, far_send, far_recv, near_send, near_recv,
):
    chunks, _, rows, width = k_buf.shape
    me = lax.axis_index("ctx")
    odd = lax.rem(me, 2)
    even = odd == 0
    partner = me + 1 - 2 * odd
    has_far_target = me + 2 < n
    has_far_source = me >= 2
    has_near_source = me >= 1
    hbm = (k_hbm, v_hbm)
    bufs = (k_buf, v_buf)

    def columns(c):
        return pl.ds(pl.multiple_of(c * width, width), width)

    def far(c, t):
        return pltpu.make_async_remote_copy(
            src_ref=hbm[t].at[:, columns(c)], dst_ref=bufs[t].at[c, 0],
            send_sem=far_send.at[c, t], recv_sem=far_recv.at[c, t],
            device_id={"ctx": lax.rem(me + 2, n)}, device_id_type=MESH)

    def near(c, t):
        return pltpu.make_async_remote_copy(
            src_ref=hbm[t].at[:, columns(c)], dst_ref=bufs[t].at[c, 1],
            send_sem=near_send.at[c, t], recv_sem=near_recv.at[c, t],
            device_id={"ctx": partner}, device_id_type=MESH)

    def relay(c, t):
        return pltpu.make_async_remote_copy(
            src_ref=bufs[t].at[c, 0], dst_ref=bufs[t].at[c, 1],
            send_sem=near_send.at[c, t], recv_sem=near_recv.at[c, t],
            device_id={"ctx": partner}, device_id_type=MESH)

    local = [
        pltpu.make_async_copy(source, target, in_sem.at[i])
        for i, (source, target) in enumerate(((q_hbm, q_own), (k_hbm, k_own), (v_hbm, v_own)))
    ]

    barrier = pltpu.get_barrier_semaphore()
    pl.semaphore_signal(barrier, inc=1, device_id={"ctx": partner}, device_id_type=MESH)

    @pl.when(has_far_target)
    def _():
        pl.semaphore_signal(barrier, inc=1, device_id={"ctx": lax.rem(me + 2, n)}, device_id_type=MESH)

    @pl.when(has_far_source)
    def _():
        pl.semaphore_signal(barrier, inc=1, device_id={"ctx": lax.rem(me + n - 2, n)}, device_id_type=MESH)

    pl.semaphore_wait(barrier, 1 + has_far_target.astype(jnp.int32) + has_far_source.astype(jnp.int32))

    def start_far(c):
        @pl.when(has_far_target)
        def _():
            for t in range(2):
                far(c, t).start()

    @pl.when(even)
    def _():
        def start_own(c, carry):
            for t in range(2):
                near(c, t).start()
            start_far(c)
            return carry
        lax.fori_loop(0, chunks, start_own, 0)

    @pl.when(odd == 1)
    def _():
        def start_own(c, carry):
            start_far(c)
            return carry
        lax.fori_loop(0, AHEAD_ODD, start_own, 0)

    for copy in local:
        copy.start()

    query = lax.broadcasted_iota(jnp.int32, (rows, KV_STEPS * rows), 0)
    key = lax.broadcasted_iota(jnp.int32, (rows, KV_STEPS * rows), 1)
    back = KV_STEPS - 1 - key // rows
    allowed = (back <= me) & ((back > 0) | (key - (KV_STEPS - 1) * rows <= query))
    bias[...] = jnp.where(allowed, 0.0, -jnp.inf)
    factor = math.log2(math.e) / math.sqrt(HEAD_DIM)

    for copy in local:
        copy.wait()

    def step(c, carry):
        @pl.when(has_far_source)
        def _():
            for t in range(2):
                far(c, t).wait_recv()

            @pl.when(odd == 1)
            def _():
                for t in range(2):
                    relay(c, t).start()

        @pl.when((odd == 1) & (c + AHEAD_ODD < chunks))
        def _():
            start_far(c + AHEAD_ODD)

        @pl.when(has_near_source)
        def _():
            for t in range(2):
                near(c, t).wait_recv()

        @pl.when(jnp.logical_not(has_far_source))
        def _():
            k_buf[c, 0] = jnp.zeros((rows, width), jnp.bfloat16)
            v_buf[c, 0] = jnp.zeros((rows, width), jnp.bfloat16)

        @pl.when(jnp.logical_not(has_near_source))
        def _():
            k_buf[c, 1] = jnp.zeros((rows, width), jnp.bfloat16)
            v_buf[c, 1] = jnp.zeros((rows, width), jnp.bfloat16)

        for h in range(width // HEAD_DIM):
            cols = slice(h * HEAD_DIM, (h + 1) * HEAD_DIM)
            place = pl.ds(pl.multiple_of(c * width + h * HEAD_DIM, HEAD_DIM), HEAD_DIM)
            q = q_own[:, place]
            k = k_buf[c, :, :, cols].reshape((KV_STEPS - 1) * rows, HEAD_DIM)
            v = v_buf[c, :, :, cols].reshape((KV_STEPS - 1) * rows, HEAD_DIM)
            s = jnp.concatenate([
                lax.dot_general(q, block, (((1,), (1,)), ((), ())), preferred_element_type=jnp.float32)
                for block in (k, k_own[:, place])], axis=1) + bias[...]
            m = jnp.max(s, axis=1, keepdims=True)
            w = jnp.exp2((s - m) * factor)
            total = jnp.sum(w, axis=1, keepdims=True)
            w = w.astype(jnp.bfloat16)
            split = (KV_STEPS - 1) * rows
            mixed = jnp.dot(w[:, :split], v, preferred_element_type=jnp.float32)
            mixed += jnp.dot(w[:, split:], v_own[:, place], preferred_element_type=jnp.float32)
            o_ref[:, place] = (mixed / total).astype(o_ref.dtype)
            lse = m * (1.0 / math.sqrt(HEAD_DIM)) + jnp.log(total)
            diagonal = (lax.broadcasted_iota(jnp.int32, (rows, rows), 0)
                        == lax.broadcasted_iota(jnp.int32, (rows, rows), 1))
            lse_ref[pl.ds(c * (width // HEAD_DIM) + h, 1), :] = jnp.sum(
                jnp.where(diagonal, lse, 0.0), axis=0, keepdims=True)
        return carry

    lax.fori_loop(0, chunks, step, 0)

    def finish(c, carry):
        @pl.when(has_far_target)
        def _():
            for t in range(2):
                far(c, t).wait_send()

        @pl.when(even | has_far_source)
        def _():
            for t in range(2):
                near(c, t).wait_send()
        return carry

    lax.fori_loop(0, chunks, finish, 0)


def shards(n, att_query, att_key, att_value):
    rows, total_width = att_query.shape
    heads = total_width // HEAD_DIM
    chunk_heads = math.gcd(heads, CHUNK_HEADS)
    chunks, width = heads // chunk_heads, chunk_heads * HEAD_DIM
    bf16 = att_query.dtype
    return pl.pallas_call(
        functools.partial(kernel, n),
        out_shape=(
            pltpu.VMEM((rows, total_width), bf16),
            pltpu.VMEM((heads, rows), jnp.float32),
        ),
        in_specs=[pl.BlockSpec(memory_space=pltpu.HBM)] * 3,
        out_specs=(pl.BlockSpec(memory_space=pltpu.VMEM), pl.BlockSpec(memory_space=pltpu.VMEM)),
        scratch_shapes=[
            pltpu.VMEM((rows, total_width), bf16),
            pltpu.VMEM((rows, total_width), bf16),
            pltpu.VMEM((rows, total_width), bf16),
            pltpu.VMEM((chunks, KV_STEPS - 1, rows, width), bf16),
            pltpu.VMEM((chunks, KV_STEPS - 1, rows, width), bf16),
            pltpu.VMEM((rows, KV_STEPS * rows), jnp.float32),
            pltpu.SemaphoreType.DMA((3,)),
            pltpu.SemaphoreType.DMA((chunks, 2)),
            pltpu.SemaphoreType.DMA((chunks, 2)),
            pltpu.SemaphoreType.DMA((chunks, 2)),
            pltpu.SemaphoreType.DMA((chunks, 2)),
        ],
        compiler_params=pltpu.CompilerParams(
            collective_id=0, has_side_effects=True, vmem_limit_bytes=32 * 1024 * 1024),
        cost_estimate=pl.CostEstimate(
            flops=4 * rows * rows * KV_STEPS * total_width,
            bytes_accessed=8 * rows * total_width,
            transcendentals=rows * rows * KV_STEPS * heads),
    )(*(pltpu.with_memory_space_constraint(x, pltpu.HBM) for x in (att_query, att_key, att_value)))


def solution(mesh):
    spec = P(("dp", "ctx"), None)
    return jax.shard_map(
        functools.partial(shards, mesh.shape["ctx"]),
        mesh=mesh,
        in_specs=(spec, spec, spec),
        out_specs=(spec, P(None, ("dp", "ctx"))),
        check_vma=False,
    )
```

```python
import functools
import math

import jax
import jax.numpy as jnp
from jax import lax
from jax.experimental import pallas as pl
from jax.experimental.pallas import tpu as pltpu
from jax.sharding import PartitionSpec as P

HEAD_DIM = 128
KV_STEPS = 3
PLAN = (1, 1, 2, 2, 2, 4, 4, 4, 4, 2, 2, 2, 1, 1)
AHEAD_ODD = 2
MESH = pl.DeviceIdType.MESH


def chunks_of(heads):
    plan = PLAN if sum(PLAN) == heads else (1,) * heads
    starts = [sum(plan[:c]) for c in range(len(plan))]
    return tuple(zip(starts, plan))


def kernel(
    n, chunks, q_hbm, k_hbm, v_hbm, o_ref, lse_ref,
    q_own, k_own, v_own, k_buf, v_buf, bias,
    in_sem, far_send, far_recv, near_send, near_recv,
):
    _, rows, _ = k_buf.shape
    count = len(chunks)
    me = lax.axis_index("ctx")
    odd = lax.rem(me, 2) == 1
    even = jnp.logical_not(odd)
    partner = me + 1 - 2 * lax.rem(me, 2)
    has_far_target = me + 2 < n
    has_far_source = me >= 2
    has_near_source = me >= 1
    hbm = (k_hbm, v_hbm)
    bufs = (k_buf, v_buf)

    def columns(c):
        start, size = chunks[c]
        return pl.ds(start * HEAD_DIM, size * HEAD_DIM)

    def far(c, t):
        return pltpu.make_async_remote_copy(
            src_ref=hbm[t].at[:, columns(c)], dst_ref=bufs[t].at[0, :, columns(c)],
            send_sem=far_send.at[c, t], recv_sem=far_recv.at[c, t],
            device_id={"ctx": lax.rem(me + 2, n)}, device_id_type=MESH)

    def near(c, t):
        return pltpu.make_async_remote_copy(
            src_ref=hbm[t].at[:, columns(c)], dst_ref=bufs[t].at[1, :, columns(c)],
            send_sem=near_send.at[c, t], recv_sem=near_recv.at[c, t],
            device_id={"ctx": partner}, device_id_type=MESH)

    def relay(c, t):
        return pltpu.make_async_remote_copy(
            src_ref=bufs[t].at[0, :, columns(c)], dst_ref=bufs[t].at[1, :, columns(c)],
            send_sem=near_send.at[c, t], recv_sem=near_recv.at[c, t],
            device_id={"ctx": partner}, device_id_type=MESH)

    local = [
        pltpu.make_async_copy(source, target, in_sem.at[i])
        for i, (source, target) in enumerate(((q_hbm, q_own), (k_hbm, k_own), (v_hbm, v_own)))
    ]

    barrier = pltpu.get_barrier_semaphore()
    pl.semaphore_signal(barrier, inc=1, device_id={"ctx": partner}, device_id_type=MESH)

    @pl.when(has_far_target)
    def _():
        pl.semaphore_signal(barrier, inc=1, device_id={"ctx": lax.rem(me + 2, n)}, device_id_type=MESH)

    @pl.when(has_far_source)
    def _():
        pl.semaphore_signal(barrier, inc=1, device_id={"ctx": lax.rem(me + n - 2, n)}, device_id_type=MESH)

    pl.semaphore_wait(barrier, 1 + has_far_target.astype(jnp.int32) + has_far_source.astype(jnp.int32))

    def start_far(c):
        for t in range(2):
            far(c, t).start()

    @pl.when(even)
    def _():
        for c in range(count):
            for t in range(2):
                near(c, t).start()

            @pl.when(has_far_target)
            def _():
                start_far(c)

    @pl.when(odd & has_far_target)
    def _():
        for c in range(AHEAD_ODD):
            start_far(c)

    for copy in local:
        copy.start()

    @pl.when(jnp.logical_not(has_far_source))
    def _():
        k_buf[0] = jnp.zeros(k_buf.shape[1:], k_buf.dtype)
        v_buf[0] = jnp.zeros(v_buf.shape[1:], v_buf.dtype)

    @pl.when(jnp.logical_not(has_near_source))
    def _():
        k_buf[1] = jnp.zeros(k_buf.shape[1:], k_buf.dtype)
        v_buf[1] = jnp.zeros(v_buf.shape[1:], v_buf.dtype)

    query = lax.broadcasted_iota(jnp.int32, (rows, KV_STEPS * rows), 0)
    key = lax.broadcasted_iota(jnp.int32, (rows, KV_STEPS * rows), 1)
    back = KV_STEPS - 1 - key // rows
    allowed = (back <= me) & ((back > 0) | (key - (KV_STEPS - 1) * rows <= query))
    bias[...] = jnp.where(allowed, 0.0, -jnp.inf)
    factor = math.log2(math.e) / math.sqrt(HEAD_DIM)

    for copy in local:
        copy.wait()

    def head(h, carry):
        place = pl.ds(pl.multiple_of(h * HEAD_DIM, HEAD_DIM), HEAD_DIM)
        q = q_own[:, place]
        k = k_buf[:, :, place].reshape((KV_STEPS - 1) * rows, HEAD_DIM)
        v = v_buf[:, :, place].reshape((KV_STEPS - 1) * rows, HEAD_DIM)
        s = jnp.concatenate([
            lax.dot_general(q, block, (((1,), (1,)), ((), ())), preferred_element_type=jnp.float32)
            for block in (k, k_own[:, place])], axis=1) + bias[...]
        m = jnp.max(s, axis=1, keepdims=True)
        w = jnp.exp2((s - m) * factor)
        total = jnp.sum(w, axis=1, keepdims=True)
        w = w.astype(jnp.bfloat16)
        split = (KV_STEPS - 1) * rows
        mixed = jnp.dot(w[:, :split], v, preferred_element_type=jnp.float32)
        mixed += jnp.dot(w[:, split:], v_own[:, place], preferred_element_type=jnp.float32)
        o_ref[:, place] = (mixed / total).astype(o_ref.dtype)
        lse = m * (1.0 / math.sqrt(HEAD_DIM)) + jnp.log(total)
        diagonal = (lax.broadcasted_iota(jnp.int32, (rows, rows), 0)
                    == lax.broadcasted_iota(jnp.int32, (rows, rows), 1))
        lse_ref[pl.ds(h, 1), :] = jnp.sum(jnp.where(diagonal, lse, 0.0), axis=0, keepdims=True)
        return carry

    def finish_chunk(c):
        @pl.when(even & has_far_source)
        def _():
            for t in range(2):
                far(c, t).wait_recv()

        @pl.when(has_near_source)
        def _():
            for t in range(2):
                near(c, t).wait_recv()

        start, size = chunks[c]
        lax.fori_loop(start, start + size, head, 0)

    for c in range(count):
        @pl.when(odd & has_far_source)
        def _():
            for t in range(2):
                far(c, t).wait_recv()
                relay(c, t).start()

        if c + AHEAD_ODD < count:
            @pl.when(odd & has_far_target)
            def _():
                start_far(c + AHEAD_ODD)

        if c >= 1:
            finish_chunk(c - 1)
    finish_chunk(count - 1)

    @pl.when(has_far_target)
    def _():
        for c in range(count):
            for t in range(2):
                far(c, t).wait_send()

    @pl.when(even | has_far_source)
    def _():
        for c in range(count):
            for t in range(2):
                near(c, t).wait_send()


def shards(n, att_query, att_key, att_value):
    rows, total_width = att_query.shape
    heads = total_width // HEAD_DIM
    chunks = chunks_of(heads)
    count = len(chunks)
    bf16 = att_query.dtype
    return pl.pallas_call(
        functools.partial(kernel, n, chunks),
        out_shape=(
            pltpu.VMEM((rows, total_width), bf16),
            pltpu.VMEM((heads, rows), jnp.float32),
        ),
        in_specs=[pl.BlockSpec(memory_space=pltpu.HBM)] * 3,
        out_specs=(pl.BlockSpec(memory_space=pltpu.VMEM), pl.BlockSpec(memory_space=pltpu.VMEM)),
        scratch_shapes=[
            pltpu.VMEM((rows, total_width), bf16),
            pltpu.VMEM((rows, total_width), bf16),
            pltpu.VMEM((rows, total_width), bf16),
            pltpu.VMEM((KV_STEPS - 1, rows, total_width), bf16),
            pltpu.VMEM((KV_STEPS - 1, rows, total_width), bf16),
            pltpu.VMEM((rows, KV_STEPS * rows), jnp.float32),
            pltpu.SemaphoreType.DMA((3,)),
            pltpu.SemaphoreType.DMA((count, 2)),
            pltpu.SemaphoreType.DMA((count, 2)),
            pltpu.SemaphoreType.DMA((count, 2)),
            pltpu.SemaphoreType.DMA((count, 2)),
        ],
        compiler_params=pltpu.CompilerParams(
            collective_id=0, has_side_effects=True, vmem_limit_bytes=32 * 1024 * 1024),
        cost_estimate=pl.CostEstimate(
            flops=4 * rows * rows * KV_STEPS * total_width,
            bytes_accessed=8 * rows * total_width,
            transcendentals=rows * rows * KV_STEPS * heads),
    )(*(pltpu.with_memory_space_constraint(x, pltpu.HBM) for x in (att_query, att_key, att_value)))


def solution(mesh):
    spec = P(("dp", "ctx"), None)
    return jax.shard_map(
        functools.partial(shards, mesh.shape["ctx"]),
        mesh=mesh,
        in_specs=(spec, spec, spec),
        out_specs=(spec, P(None, ("dp", "ctx"))),
        check_vma=False,
    )
```

```python
import functools
import math

import jax
import jax.numpy as jnp
from jax import lax
from jax.experimental import pallas as pl
from jax.experimental.pallas import tpu as pltpu
from jax.sharding import PartitionSpec as P

HEAD_DIM = 128
KV_STEPS = 3
PLAN = (1, 1, 2, 2, 2, 4, 4, 4, 4, 2, 2, 2, 1, 1)
AHEAD_ODD = 64
MESH = pl.DeviceIdType.MESH


def chunks_of(heads):
    plan = PLAN if sum(PLAN) == heads else (1,) * heads
    starts = [sum(plan[:c]) for c in range(len(plan))]
    return tuple(zip(starts, plan))


def kernel(
    n, chunks, q_hbm, k_hbm, v_hbm, o_ref, lse_ref,
    q_own, k_own, v_own, k_buf, v_buf, bias,
    in_sem, far_send, far_recv, near_send, near_recv,
):
    _, rows, _ = k_buf.shape
    count = len(chunks)
    me = lax.axis_index("ctx")
    odd = lax.rem(me, 2) == 1
    even = jnp.logical_not(odd)
    partner = me + 1 - 2 * lax.rem(me, 2)
    has_far_target = me + 2 < n
    has_far_source = me >= 2
    has_near_source = me >= 1
    hbm = (k_hbm, v_hbm)
    bufs = (k_buf, v_buf)

    def columns(c):
        start, size = chunks[c]
        return pl.ds(start * HEAD_DIM, size * HEAD_DIM)

    def far(c, t):
        return pltpu.make_async_remote_copy(
            src_ref=hbm[t].at[:, columns(c)], dst_ref=bufs[t].at[0, :, columns(c)],
            send_sem=far_send.at[c, t], recv_sem=far_recv.at[c, t],
            device_id={"ctx": lax.rem(me + 2, n)}, device_id_type=MESH)

    def near(c, t):
        return pltpu.make_async_remote_copy(
            src_ref=hbm[t].at[:, columns(c)], dst_ref=bufs[t].at[1, :, columns(c)],
            send_sem=near_send.at[c, t], recv_sem=near_recv.at[c, t],
            device_id={"ctx": partner}, device_id_type=MESH)

    def relay(c, t):
        return pltpu.make_async_remote_copy(
            src_ref=bufs[t].at[0, :, columns(c)], dst_ref=bufs[t].at[1, :, columns(c)],
            send_sem=near_send.at[c, t], recv_sem=near_recv.at[c, t],
            device_id={"ctx": partner}, device_id_type=MESH)

    local = [
        pltpu.make_async_copy(source, target, in_sem.at[i])
        for i, (source, target) in enumerate(((q_hbm, q_own), (k_hbm, k_own), (v_hbm, v_own)))
    ]

    barrier = pltpu.get_barrier_semaphore()
    pl.semaphore_signal(barrier, inc=1, device_id={"ctx": partner}, device_id_type=MESH)

    @pl.when(has_far_target)
    def _():
        pl.semaphore_signal(barrier, inc=1, device_id={"ctx": lax.rem(me + 2, n)}, device_id_type=MESH)

    @pl.when(has_far_source)
    def _():
        pl.semaphore_signal(barrier, inc=1, device_id={"ctx": lax.rem(me + n - 2, n)}, device_id_type=MESH)

    pl.semaphore_wait(barrier, 1 + has_far_target.astype(jnp.int32) + has_far_source.astype(jnp.int32))

    def start_far(c):
        for t in range(2):
            far(c, t).start()

    @pl.when(even)
    def _():
        for c in range(count):
            for t in range(2):
                near(c, t).start()

            @pl.when(has_far_target)
            def _():
                start_far(c)

    @pl.when(odd & has_far_target)
    def _():
        for c in range(min(AHEAD_ODD, count)):
            start_far(c)

    for copy in local:
        copy.start()

    @pl.when(jnp.logical_not(has_far_source))
    def _():
        k_buf[0] = jnp.zeros(k_buf.shape[1:], k_buf.dtype)
        v_buf[0] = jnp.zeros(v_buf.shape[1:], v_buf.dtype)

    @pl.when(jnp.logical_not(has_near_source))
    def _():
        k_buf[1] = jnp.zeros(k_buf.shape[1:], k_buf.dtype)
        v_buf[1] = jnp.zeros(v_buf.shape[1:], v_buf.dtype)

    query = lax.broadcasted_iota(jnp.int32, (rows, KV_STEPS * rows), 0)
    key = lax.broadcasted_iota(jnp.int32, (rows, KV_STEPS * rows), 1)
    back = KV_STEPS - 1 - key // rows
    allowed = (back <= me) & ((back > 0) | (key - (KV_STEPS - 1) * rows <= query))
    bias[...] = jnp.where(allowed, 0.0, -jnp.inf)
    factor = math.log2(math.e) / math.sqrt(HEAD_DIM)

    for copy in local:
        copy.wait()

    def head(h, carry):
        place = pl.ds(pl.multiple_of(h * HEAD_DIM, HEAD_DIM), HEAD_DIM)
        q = q_own[:, place]
        k = k_buf[:, :, place].reshape((KV_STEPS - 1) * rows, HEAD_DIM)
        v = v_buf[:, :, place].reshape((KV_STEPS - 1) * rows, HEAD_DIM)
        s = jnp.concatenate([
            lax.dot_general(q, block, (((1,), (1,)), ((), ())), preferred_element_type=jnp.float32)
            for block in (k, k_own[:, place])], axis=1) + bias[...]
        m = jnp.max(s, axis=1, keepdims=True)
        w = jnp.exp2((s - m) * factor)
        total = jnp.sum(w, axis=1, keepdims=True)
        w = w.astype(jnp.bfloat16)
        split = (KV_STEPS - 1) * rows
        mixed = jnp.dot(w[:, :split], v, preferred_element_type=jnp.float32)
        mixed += jnp.dot(w[:, split:], v_own[:, place], preferred_element_type=jnp.float32)
        o_ref[:, place] = (mixed / total).astype(o_ref.dtype)
        lse = m * (1.0 / math.sqrt(HEAD_DIM)) + jnp.log(total)
        diagonal = (lax.broadcasted_iota(jnp.int32, (rows, rows), 0)
                    == lax.broadcasted_iota(jnp.int32, (rows, rows), 1))
        lse_ref[pl.ds(h, 1), :] = jnp.sum(jnp.where(diagonal, lse, 0.0), axis=0, keepdims=True)
        return carry

    def finish_chunk(c):
        @pl.when(even & has_far_source)
        def _():
            for t in range(2):
                far(c, t).wait_recv()

        @pl.when(has_near_source)
        def _():
            for t in range(2):
                near(c, t).wait_recv()

        start, size = chunks[c]
        lax.fori_loop(start, start + size, head, 0)

    for c in range(count):
        @pl.when(odd & has_far_source)
        def _():
            for t in range(2):
                far(c, t).wait_recv()
                relay(c, t).start()

        if c + AHEAD_ODD < count:
            @pl.when(odd & has_far_target)
            def _():
                start_far(c + AHEAD_ODD)

        if c >= 1:
            finish_chunk(c - 1)
    finish_chunk(count - 1)

    @pl.when(has_far_target)
    def _():
        for c in range(count):
            for t in range(2):
                far(c, t).wait_send()

    @pl.when(even | has_far_source)
    def _():
        for c in range(count):
            for t in range(2):
                near(c, t).wait_send()


def write_kernel(o_vmem, lse_vmem, o_hbm, lse_hbm, sem):
    copies = [
        pltpu.make_async_copy(o_vmem, o_hbm, sem.at[0]),
        pltpu.make_async_copy(lse_vmem, lse_hbm, sem.at[1]),
    ]
    for copy in copies:
        copy.start()
    for copy in copies:
        copy.wait()


def write(attn_out, attn_lse):
    return pl.pallas_call(
        write_kernel,
        out_shape=(
            jax.ShapeDtypeStruct(attn_out.shape, attn_out.dtype),
            jax.ShapeDtypeStruct(attn_lse.shape, attn_lse.dtype),
        ),
        in_specs=[pl.BlockSpec(memory_space=pltpu.VMEM)] * 2,
        out_specs=(pl.BlockSpec(memory_space=pltpu.HBM),) * 2,
        scratch_shapes=[pltpu.SemaphoreType.DMA((2,))],
        compiler_params=pltpu.CompilerParams(vmem_limit_bytes=32 * 1024 * 1024),
        cost_estimate=pl.CostEstimate(
            flops=0, bytes_accessed=4 * attn_out.size, transcendentals=0),
    )(*(pltpu.with_memory_space_constraint(x, pltpu.VMEM) for x in (attn_out, attn_lse)))


def shards(n, att_query, att_key, att_value):
    rows, total_width = att_query.shape
    heads = total_width // HEAD_DIM
    chunks = chunks_of(heads)
    count = len(chunks)
    bf16 = att_query.dtype
    attn_out, attn_lse = pl.pallas_call(
        functools.partial(kernel, n, chunks),
        out_shape=(
            pltpu.VMEM((rows, total_width), bf16),
            pltpu.VMEM((heads, rows), jnp.float32),
        ),
        in_specs=[pl.BlockSpec(memory_space=pltpu.HBM)] * 3,
        out_specs=(pl.BlockSpec(memory_space=pltpu.VMEM), pl.BlockSpec(memory_space=pltpu.VMEM)),
        scratch_shapes=[
            pltpu.VMEM((rows, total_width), bf16),
            pltpu.VMEM((rows, total_width), bf16),
            pltpu.VMEM((rows, total_width), bf16),
            pltpu.VMEM((KV_STEPS - 1, rows, total_width), bf16),
            pltpu.VMEM((KV_STEPS - 1, rows, total_width), bf16),
            pltpu.VMEM((rows, KV_STEPS * rows), jnp.float32),
            pltpu.SemaphoreType.DMA((3,)),
            pltpu.SemaphoreType.DMA((count, 2)),
            pltpu.SemaphoreType.DMA((count, 2)),
            pltpu.SemaphoreType.DMA((count, 2)),
            pltpu.SemaphoreType.DMA((count, 2)),
        ],
        compiler_params=pltpu.CompilerParams(
            collective_id=0, has_side_effects=True, vmem_limit_bytes=32 * 1024 * 1024),
        cost_estimate=pl.CostEstimate(
            flops=4 * rows * rows * KV_STEPS * total_width,
            bytes_accessed=8 * rows * total_width,
            transcendentals=rows * rows * KV_STEPS * heads),
    )(*(pltpu.with_memory_space_constraint(x, pltpu.HBM) for x in (att_query, att_key, att_value)))
    return write(attn_out, attn_lse)


def solution(mesh):
    spec = P(("dp", "ctx"), None)
    return jax.shard_map(
        functools.partial(shards, mesh.shape["ctx"]),
        mesh=mesh,
        in_specs=(spec, spec, spec),
        out_specs=(spec, P(None, ("dp", "ctx"))),
        check_vma=False,
    )
```

```python
import functools
import math

import jax
import jax.numpy as jnp
from jax import lax
from jax.experimental import pallas as pl
from jax.experimental.pallas import tpu as pltpu
from jax.sharding import PartitionSpec as P

HEAD_DIM = 128
KV_STEPS = 3
CHUNK_HEADS = 1
AHEAD_ODD = 5
MESH = pl.DeviceIdType.MESH


def kernel(
    n, chunk_heads, q_hbm, k_hbm, v_hbm, o_ref, lse_ref,
    q_own, k_own, v_own, k_buf, v_buf, bias,
    in_sem, far_send, far_recv, near_send, near_recv,
):
    _, rows, total_width = k_buf.shape
    width = chunk_heads * HEAD_DIM
    count = total_width // width
    ahead = min(AHEAD_ODD, count)
    me = lax.axis_index("ctx")
    odd = lax.rem(me, 2) == 1
    even = jnp.logical_not(odd)
    partner = me + 1 - 2 * lax.rem(me, 2)
    has_far_target = me + 2 < n
    has_far_source = me >= 2
    has_near_source = me >= 1
    hbm = (k_hbm, v_hbm)
    bufs = (k_buf, v_buf)

    def columns(c):
        return pl.ds(pl.multiple_of(c * width, width), width)

    def far(c, t):
        return pltpu.make_async_remote_copy(
            src_ref=hbm[t].at[:, columns(c)], dst_ref=bufs[t].at[0, :, columns(c)],
            send_sem=far_send.at[c, t], recv_sem=far_recv.at[c, t],
            device_id={"ctx": lax.rem(me + 2, n)}, device_id_type=MESH)

    def near(c, t):
        return pltpu.make_async_remote_copy(
            src_ref=hbm[t].at[:, columns(c)], dst_ref=bufs[t].at[1, :, columns(c)],
            send_sem=near_send.at[c, t], recv_sem=near_recv.at[c, t],
            device_id={"ctx": partner}, device_id_type=MESH)

    def relay(c, t):
        return pltpu.make_async_remote_copy(
            src_ref=bufs[t].at[0, :, columns(c)], dst_ref=bufs[t].at[1, :, columns(c)],
            send_sem=near_send.at[c, t], recv_sem=near_recv.at[c, t],
            device_id={"ctx": partner}, device_id_type=MESH)

    local = [
        pltpu.make_async_copy(source, target, in_sem.at[i])
        for i, (source, target) in enumerate(((q_hbm, q_own), (k_hbm, k_own), (v_hbm, v_own)))
    ]

    barrier = pltpu.get_barrier_semaphore()
    pl.semaphore_signal(barrier, inc=1, device_id={"ctx": partner}, device_id_type=MESH)

    @pl.when(has_far_target)
    def _():
        pl.semaphore_signal(barrier, inc=1, device_id={"ctx": lax.rem(me + 2, n)}, device_id_type=MESH)

    @pl.when(has_far_source)
    def _():
        pl.semaphore_signal(barrier, inc=1, device_id={"ctx": lax.rem(me + n - 2, n)}, device_id_type=MESH)

    pl.semaphore_wait(barrier, 1 + has_far_target.astype(jnp.int32) + has_far_source.astype(jnp.int32))

    def start_far(c):
        for t in range(2):
            far(c, t).start()

    def start_near(c):
        for t in range(2):
            near(c, t).start()

    def each(start, stop, body):
        def step(c, carry):
            body(c)
            return carry
        lax.fori_loop(start, stop, step, 0)

    @pl.when(even & has_far_target)
    def _():
        def both(c):
            start_near(c)
            start_far(c)
        each(0, count, both)

    @pl.when(even & jnp.logical_not(has_far_target))
    def _():
        each(0, count, start_near)

    @pl.when(odd & has_far_target)
    def _():
        each(0, ahead, start_far)

    for copy in local:
        copy.start()

    @pl.when(jnp.logical_not(has_far_source))
    def _():
        k_buf[0] = jnp.zeros(k_buf.shape[1:], k_buf.dtype)
        v_buf[0] = jnp.zeros(v_buf.shape[1:], v_buf.dtype)

    @pl.when(jnp.logical_not(has_near_source))
    def _():
        k_buf[1] = jnp.zeros(k_buf.shape[1:], k_buf.dtype)
        v_buf[1] = jnp.zeros(v_buf.shape[1:], v_buf.dtype)

    query = lax.broadcasted_iota(jnp.int32, (rows, KV_STEPS * rows), 0)
    key = lax.broadcasted_iota(jnp.int32, (rows, KV_STEPS * rows), 1)
    back = KV_STEPS - 1 - key // rows
    allowed = (back <= me) & ((back > 0) | (key - (KV_STEPS - 1) * rows <= query))
    bias[...] = jnp.where(allowed, 0.0, -jnp.inf)
    factor = math.log2(math.e) / math.sqrt(HEAD_DIM)

    for copy in local:
        copy.wait()

    def head(h):
        place = pl.ds(pl.multiple_of(h * HEAD_DIM, HEAD_DIM), HEAD_DIM)
        q = q_own[:, place]
        k = k_buf[:, :, place].reshape((KV_STEPS - 1) * rows, HEAD_DIM)
        v = v_buf[:, :, place].reshape((KV_STEPS - 1) * rows, HEAD_DIM)
        s = jnp.concatenate([
            lax.dot_general(q, block, (((1,), (1,)), ((), ())), preferred_element_type=jnp.float32)
            for block in (k, k_own[:, place])], axis=1) + bias[...]
        m = jnp.max(s, axis=1, keepdims=True)
        w = jnp.exp2((s - m) * factor)
        total = jnp.sum(w, axis=1, keepdims=True)
        w = w.astype(jnp.bfloat16)
        split = (KV_STEPS - 1) * rows
        mixed = jnp.dot(w[:, :split], v, preferred_element_type=jnp.float32)
        mixed += jnp.dot(w[:, split:], v_own[:, place], preferred_element_type=jnp.float32)
        o_ref[:, place] = (mixed / total).astype(o_ref.dtype)
        lse = m * (1.0 / math.sqrt(HEAD_DIM)) + jnp.log(total)
        diagonal = (lax.broadcasted_iota(jnp.int32, (rows, rows), 0)
                    == lax.broadcasted_iota(jnp.int32, (rows, rows), 1))
        lse_ref[pl.ds(h, 1), :] = jnp.sum(jnp.where(diagonal, lse, 0.0), axis=0, keepdims=True)

    def finish_chunk(c):
        @pl.when(even & has_far_source)
        def _():
            for t in range(2):
                far(c, t).wait_recv()

        @pl.when(has_near_source)
        def _():
            for t in range(2):
                near(c, t).wait_recv()

        for h in range(chunk_heads):
            head(c * chunk_heads + h)

    def step(c):
        @pl.when(odd & has_far_source)
        def _():
            for t in range(2):
                far(c, t).wait_recv()
                relay(c, t).start()

        @pl.when(odd & has_far_target & (c + ahead < count))
        def _():
            start_far(c + ahead)

        @pl.when(c >= 1)
        def _():
            finish_chunk(c - 1)

    each(0, count, step)
    finish_chunk(count - 1)

    @pl.when(has_far_target)
    def _():
        def body(c):
            for t in range(2):
                far(c, t).wait_send()
        each(0, count, body)

    @pl.when(even | has_far_source)
    def _():
        def body(c):
            for t in range(2):
                near(c, t).wait_send()
        each(0, count, body)


def write_kernel(o_vmem, lse_vmem, o_hbm, lse_hbm, sem):
    copies = [
        pltpu.make_async_copy(o_vmem, o_hbm, sem.at[0]),
        pltpu.make_async_copy(lse_vmem, lse_hbm, sem.at[1]),
    ]
    for copy in copies:
        copy.start()
    for copy in copies:
        copy.wait()


def write(attn_out, attn_lse):
    return pl.pallas_call(
        write_kernel,
        out_shape=(
            jax.ShapeDtypeStruct(attn_out.shape, attn_out.dtype),
            jax.ShapeDtypeStruct(attn_lse.shape, attn_lse.dtype),
        ),
        in_specs=[pl.BlockSpec(memory_space=pltpu.VMEM)] * 2,
        out_specs=(pl.BlockSpec(memory_space=pltpu.HBM),) * 2,
        scratch_shapes=[pltpu.SemaphoreType.DMA((2,))],
        compiler_params=pltpu.CompilerParams(vmem_limit_bytes=32 * 1024 * 1024),
        cost_estimate=pl.CostEstimate(
            flops=0, bytes_accessed=4 * attn_out.size, transcendentals=0),
    )(*(pltpu.with_memory_space_constraint(x, pltpu.VMEM) for x in (attn_out, attn_lse)))


def shards(n, att_query, att_key, att_value):
    rows, total_width = att_query.shape
    heads = total_width // HEAD_DIM
    chunk_heads = math.gcd(heads, CHUNK_HEADS)
    count = heads // chunk_heads
    bf16 = att_query.dtype
    attn_out, attn_lse = pl.pallas_call(
        functools.partial(kernel, n, chunk_heads),
        out_shape=(
            pltpu.VMEM((rows, total_width), bf16),
            pltpu.VMEM((heads, rows), jnp.float32),
        ),
        in_specs=[pl.BlockSpec(memory_space=pltpu.HBM)] * 3,
        out_specs=(pl.BlockSpec(memory_space=pltpu.VMEM), pl.BlockSpec(memory_space=pltpu.VMEM)),
        scratch_shapes=[
            pltpu.VMEM((rows, total_width), bf16),
            pltpu.VMEM((rows, total_width), bf16),
            pltpu.VMEM((rows, total_width), bf16),
            pltpu.VMEM((KV_STEPS - 1, rows, total_width), bf16),
            pltpu.VMEM((KV_STEPS - 1, rows, total_width), bf16),
            pltpu.VMEM((rows, KV_STEPS * rows), jnp.float32),
            pltpu.SemaphoreType.DMA((3,)),
            pltpu.SemaphoreType.DMA((count, 2)),
            pltpu.SemaphoreType.DMA((count, 2)),
            pltpu.SemaphoreType.DMA((count, 2)),
            pltpu.SemaphoreType.DMA((count, 2)),
        ],
        compiler_params=pltpu.CompilerParams(
            collective_id=0, has_side_effects=True, vmem_limit_bytes=32 * 1024 * 1024),
        cost_estimate=pl.CostEstimate(
            flops=4 * rows * rows * KV_STEPS * total_width,
            bytes_accessed=8 * rows * total_width,
            transcendentals=rows * rows * KV_STEPS * heads),
    )(*(pltpu.with_memory_space_constraint(x, pltpu.HBM) for x in (att_query, att_key, att_value)))
    return write(attn_out, attn_lse)


def solution(mesh):
    spec = P(("dp", "ctx"), None)
    return jax.shard_map(
        functools.partial(shards, mesh.shape["ctx"]),
        mesh=mesh,
        in_specs=(spec, spec, spec),
        out_specs=(spec, P(None, ("dp", "ctx"))),
        check_vma=False,
    )
```

```python
import functools
import math

import jax
import jax.numpy as jnp
from jax import lax
from jax.experimental import pallas as pl
from jax.experimental.pallas import tpu as pltpu
from jax.sharding import PartitionSpec as P

HEAD_DIM = 128
KV_STEPS = 3
CHUNK_HEADS = 2
AHEAD_ODD = 3
MESH = pl.DeviceIdType.MESH


def kernel(
    n, chunk_heads, q_hbm, k_hbm, v_hbm, o_ref, lse_ref,
    q_own, k_own, v_own, k_buf, v_buf, bias,
    in_sem, far_send, far_recv, near_send, near_recv,
):
    _, rows, total_width = k_buf.shape
    width = chunk_heads * HEAD_DIM
    count = total_width // width
    ahead = min(AHEAD_ODD, count)
    me = lax.axis_index("ctx")
    odd = lax.rem(me, 2) == 1
    even = jnp.logical_not(odd)
    partner = me + 1 - 2 * lax.rem(me, 2)
    has_far_target = me + 2 < n
    has_far_source = me >= 2
    has_near_source = me >= 1
    hbm = (k_hbm, v_hbm)
    bufs = (k_buf, v_buf)

    def columns(c):
        return pl.ds(pl.multiple_of(c * width, width), width)

    def far(c, t):
        return pltpu.make_async_remote_copy(
            src_ref=hbm[t].at[:, columns(c)], dst_ref=bufs[t].at[0, :, columns(c)],
            send_sem=far_send.at[c, t], recv_sem=far_recv.at[c, t],
            device_id={"ctx": lax.rem(me + 2, n)}, device_id_type=MESH)

    def near(c, t):
        return pltpu.make_async_remote_copy(
            src_ref=hbm[t].at[:, columns(c)], dst_ref=bufs[t].at[1, :, columns(c)],
            send_sem=near_send.at[c, t], recv_sem=near_recv.at[c, t],
            device_id={"ctx": partner}, device_id_type=MESH)

    def relay(c, t):
        return pltpu.make_async_remote_copy(
            src_ref=bufs[t].at[0, :, columns(c)], dst_ref=bufs[t].at[1, :, columns(c)],
            send_sem=near_send.at[c, t], recv_sem=near_recv.at[c, t],
            device_id={"ctx": partner}, device_id_type=MESH)

    local = [
        pltpu.make_async_copy(source, target, in_sem.at[i])
        for i, (source, target) in enumerate(((q_hbm, q_own), (k_hbm, k_own), (v_hbm, v_own)))
    ]

    barrier = pltpu.get_barrier_semaphore()
    pl.semaphore_signal(barrier, inc=1, device_id={"ctx": partner}, device_id_type=MESH)

    @pl.when(has_far_target)
    def _():
        pl.semaphore_signal(barrier, inc=1, device_id={"ctx": lax.rem(me + 2, n)}, device_id_type=MESH)

    @pl.when(has_far_source)
    def _():
        pl.semaphore_signal(barrier, inc=1, device_id={"ctx": lax.rem(me + n - 2, n)}, device_id_type=MESH)

    pl.semaphore_wait(barrier, 1 + has_far_target.astype(jnp.int32) + has_far_source.astype(jnp.int32))

    def start_far(c):
        for t in range(2):
            far(c, t).start()

    def start_near(c):
        for t in range(2):
            near(c, t).start()

    def each(start, stop, body):
        def step(c, carry):
            body(c)
            return carry
        lax.fori_loop(start, stop, step, 0)

    @pl.when(even & has_far_target)
    def _():
        def both(c):
            start_near(c)
            start_far(c)
        each(0, count, both)

    @pl.when(even & jnp.logical_not(has_far_target))
    def _():
        each(0, count, start_near)

    @pl.when(odd & has_far_target)
    def _():
        each(0, ahead, start_far)

    for copy in local:
        copy.start()

    @pl.when(jnp.logical_not(has_far_source))
    def _():
        k_buf[0] = jnp.zeros(k_buf.shape[1:], k_buf.dtype)
        v_buf[0] = jnp.zeros(v_buf.shape[1:], v_buf.dtype)

    @pl.when(jnp.logical_not(has_near_source))
    def _():
        k_buf[1] = jnp.zeros(k_buf.shape[1:], k_buf.dtype)
        v_buf[1] = jnp.zeros(v_buf.shape[1:], v_buf.dtype)

    query = lax.broadcasted_iota(jnp.int32, (rows, KV_STEPS * rows), 0)
    key = lax.broadcasted_iota(jnp.int32, (rows, KV_STEPS * rows), 1)
    back = KV_STEPS - 1 - key // rows
    allowed = (back <= me) & ((back > 0) | (key - (KV_STEPS - 1) * rows <= query))
    bias[...] = jnp.where(allowed, 0.0, -jnp.inf)
    factor = math.log2(math.e) / math.sqrt(HEAD_DIM)

    for copy in local:
        copy.wait()

    def head(h):
        place = pl.ds(pl.multiple_of(h * HEAD_DIM, HEAD_DIM), HEAD_DIM)
        q = q_own[:, place]
        k = k_buf[:, :, place].reshape((KV_STEPS - 1) * rows, HEAD_DIM)
        v = v_buf[:, :, place].reshape((KV_STEPS - 1) * rows, HEAD_DIM)
        s = jnp.concatenate([
            lax.dot_general(q, block, (((1,), (1,)), ((), ())), preferred_element_type=jnp.float32)
            for block in (k, k_own[:, place])], axis=1) + bias[...]
        m = jnp.max(s, axis=1, keepdims=True)
        w = jnp.exp2((s - m) * factor)
        total = jnp.sum(w, axis=1, keepdims=True)
        w = w.astype(jnp.bfloat16)
        split = (KV_STEPS - 1) * rows
        mixed = jnp.dot(w[:, :split], v, preferred_element_type=jnp.float32)
        mixed += jnp.dot(w[:, split:], v_own[:, place], preferred_element_type=jnp.float32)
        o_ref[:, place] = (mixed / total).astype(o_ref.dtype)
        lse = m * (1.0 / math.sqrt(HEAD_DIM)) + jnp.log(total)
        diagonal = (lax.broadcasted_iota(jnp.int32, (rows, rows), 0)
                    == lax.broadcasted_iota(jnp.int32, (rows, rows), 1))
        lse_ref[pl.ds(h, 1), :] = jnp.sum(jnp.where(diagonal, lse, 0.0), axis=0, keepdims=True)

    def finish_chunk(c):
        @pl.when(even & has_far_source)
        def _():
            for t in range(2):
                far(c, t).wait_recv()

        @pl.when(has_near_source)
        def _():
            for t in range(2):
                near(c, t).wait_recv()

        for h in range(chunk_heads):
            head(c * chunk_heads + h)

    def step(c):
        @pl.when(odd & has_far_source)
        def _():
            for t in range(2):
                far(c, t).wait_recv()
                relay(c, t).start()

        @pl.when(odd & has_far_target & (c + ahead < count))
        def _():
            start_far(c + ahead)

        @pl.when(c >= 1)
        def _():
            finish_chunk(c - 1)

    each(0, count, step)
    finish_chunk(count - 1)

    @pl.when(has_far_target)
    def _():
        def body(c):
            for t in range(2):
                far(c, t).wait_send()
        each(0, count, body)

    @pl.when(even | has_far_source)
    def _():
        def body(c):
            for t in range(2):
                near(c, t).wait_send()
        each(0, count, body)


def write_kernel(o_vmem, lse_vmem, o_hbm, lse_hbm, sem):
    copies = [
        pltpu.make_async_copy(o_vmem, o_hbm, sem.at[0]),
        pltpu.make_async_copy(lse_vmem, lse_hbm, sem.at[1]),
    ]
    for copy in copies:
        copy.start()
    for copy in copies:
        copy.wait()


def write(attn_out, attn_lse):
    return pl.pallas_call(
        write_kernel,
        out_shape=(
            jax.ShapeDtypeStruct(attn_out.shape, attn_out.dtype),
            jax.ShapeDtypeStruct(attn_lse.shape, attn_lse.dtype),
        ),
        in_specs=[pl.BlockSpec(memory_space=pltpu.VMEM)] * 2,
        out_specs=(pl.BlockSpec(memory_space=pltpu.HBM),) * 2,
        scratch_shapes=[pltpu.SemaphoreType.DMA((2,))],
        compiler_params=pltpu.CompilerParams(vmem_limit_bytes=32 * 1024 * 1024),
        cost_estimate=pl.CostEstimate(
            flops=0, bytes_accessed=4 * attn_out.size, transcendentals=0),
    )(*(pltpu.with_memory_space_constraint(x, pltpu.VMEM) for x in (attn_out, attn_lse)))


def shards(n, att_query, att_key, att_value):
    rows, total_width = att_query.shape
    heads = total_width // HEAD_DIM
    chunk_heads = math.gcd(heads, CHUNK_HEADS)
    count = heads // chunk_heads
    bf16 = att_query.dtype
    attn_out, attn_lse = pl.pallas_call(
        functools.partial(kernel, n, chunk_heads),
        out_shape=(
            pltpu.VMEM((rows, total_width), bf16),
            pltpu.VMEM((heads, rows), jnp.float32),
        ),
        in_specs=[pl.BlockSpec(memory_space=pltpu.HBM)] * 3,
        out_specs=(pl.BlockSpec(memory_space=pltpu.VMEM), pl.BlockSpec(memory_space=pltpu.VMEM)),
        scratch_shapes=[
            pltpu.VMEM((rows, total_width), bf16),
            pltpu.VMEM((rows, total_width), bf16),
            pltpu.VMEM((rows, total_width), bf16),
            pltpu.VMEM((KV_STEPS - 1, rows, total_width), bf16),
            pltpu.VMEM((KV_STEPS - 1, rows, total_width), bf16),
            pltpu.VMEM((rows, KV_STEPS * rows), jnp.float32),
            pltpu.SemaphoreType.DMA((3,)),
            pltpu.SemaphoreType.DMA((count, 2)),
            pltpu.SemaphoreType.DMA((count, 2)),
            pltpu.SemaphoreType.DMA((count, 2)),
            pltpu.SemaphoreType.DMA((count, 2)),
        ],
        compiler_params=pltpu.CompilerParams(
            collective_id=0, has_side_effects=True, vmem_limit_bytes=32 * 1024 * 1024),
        cost_estimate=pl.CostEstimate(
            flops=4 * rows * rows * KV_STEPS * total_width,
            bytes_accessed=8 * rows * total_width,
            transcendentals=rows * rows * KV_STEPS * heads),
    )(*(pltpu.with_memory_space_constraint(x, pltpu.HBM) for x in (att_query, att_key, att_value)))
    return write(attn_out, attn_lse)


def solution(mesh):
    spec = P(("dp", "ctx"), None)
    return jax.shard_map(
        functools.partial(shards, mesh.shape["ctx"]),
        mesh=mesh,
        in_specs=(spec, spec, spec),
        out_specs=(spec, P(None, ("dp", "ctx"))),
        check_vma=False,
    )
```

```python
import functools
import math

import jax
import jax.numpy as jnp
from jax import lax
from jax.experimental import pallas as pl
from jax.experimental.pallas import tpu as pltpu
from jax.sharding import PartitionSpec as P

HEAD_DIM = 128
KV_STEPS = 3
CHUNK_HEADS = 2
AHEAD_ODD = 3
LAG = 2
MESH = pl.DeviceIdType.MESH


def kernel(
    n, chunk_heads, q_hbm, k_hbm, v_hbm, o_ref, lse_ref,
    q_own, k_own, v_own, k_buf, v_buf, bias,
    in_sem, far_send, far_recv, near_send, near_recv,
):
    _, rows, total_width = k_buf.shape
    width = chunk_heads * HEAD_DIM
    count = total_width // width
    ahead = min(AHEAD_ODD, count)
    me = lax.axis_index("ctx")
    odd = lax.rem(me, 2) == 1
    even = jnp.logical_not(odd)
    partner = me + 1 - 2 * lax.rem(me, 2)
    has_far_target = me + 2 < n
    has_far_source = me >= 2
    has_near_source = me >= 1
    hbm = (k_hbm, v_hbm)
    bufs = (k_buf, v_buf)

    def columns(c):
        return pl.ds(pl.multiple_of(c * width, width), width)

    def far(c, t):
        return pltpu.make_async_remote_copy(
            src_ref=hbm[t].at[:, columns(c)], dst_ref=bufs[t].at[0, :, columns(c)],
            send_sem=far_send.at[c, t], recv_sem=far_recv.at[c, t],
            device_id={"ctx": lax.rem(me + 2, n)}, device_id_type=MESH)

    def near(c, t):
        return pltpu.make_async_remote_copy(
            src_ref=hbm[t].at[:, columns(c)], dst_ref=bufs[t].at[1, :, columns(c)],
            send_sem=near_send.at[c, t], recv_sem=near_recv.at[c, t],
            device_id={"ctx": partner}, device_id_type=MESH)

    def relay(c, t):
        return pltpu.make_async_remote_copy(
            src_ref=bufs[t].at[0, :, columns(c)], dst_ref=bufs[t].at[1, :, columns(c)],
            send_sem=near_send.at[c, t], recv_sem=near_recv.at[c, t],
            device_id={"ctx": partner}, device_id_type=MESH)

    local = [
        pltpu.make_async_copy(source, target, in_sem.at[i])
        for i, (source, target) in enumerate(((q_hbm, q_own), (k_hbm, k_own), (v_hbm, v_own)))
    ]

    barrier = pltpu.get_barrier_semaphore()
    pl.semaphore_signal(barrier, inc=1, device_id={"ctx": partner}, device_id_type=MESH)

    @pl.when(has_far_target)
    def _():
        pl.semaphore_signal(barrier, inc=1, device_id={"ctx": lax.rem(me + 2, n)}, device_id_type=MESH)

    @pl.when(has_far_source)
    def _():
        pl.semaphore_signal(barrier, inc=1, device_id={"ctx": lax.rem(me + n - 2, n)}, device_id_type=MESH)

    pl.semaphore_wait(barrier, 1 + has_far_target.astype(jnp.int32) + has_far_source.astype(jnp.int32))

    def start_far(c):
        for t in range(2):
            far(c, t).start()

    def start_near(c):
        for t in range(2):
            near(c, t).start()

    def each(start, stop, body):
        def step(c, carry):
            body(c)
            return carry
        lax.fori_loop(start, stop, step, 0)

    @pl.when(even & has_far_target)
    def _():
        def both(c):
            start_near(c)
            start_far(c)
        each(0, count, both)

    @pl.when(even & jnp.logical_not(has_far_target))
    def _():
        each(0, count, start_near)

    @pl.when(odd & has_far_target)
    def _():
        each(0, ahead, start_far)

    for copy in local:
        copy.start()

    @pl.when(jnp.logical_not(has_far_source))
    def _():
        k_buf[0] = jnp.zeros(k_buf.shape[1:], k_buf.dtype)
        v_buf[0] = jnp.zeros(v_buf.shape[1:], v_buf.dtype)

    @pl.when(jnp.logical_not(has_near_source))
    def _():
        k_buf[1] = jnp.zeros(k_buf.shape[1:], k_buf.dtype)
        v_buf[1] = jnp.zeros(v_buf.shape[1:], v_buf.dtype)

    query = lax.broadcasted_iota(jnp.int32, (rows, KV_STEPS * rows), 0)
    key = lax.broadcasted_iota(jnp.int32, (rows, KV_STEPS * rows), 1)
    back = KV_STEPS - 1 - key // rows
    allowed = (back <= me) & ((back > 0) | (key - (KV_STEPS - 1) * rows <= query))
    bias[...] = jnp.where(allowed, 0.0, -jnp.inf)
    factor = math.log2(math.e) / math.sqrt(HEAD_DIM)

    for copy in local:
        copy.wait()

    def scores(q, block, columns_of_bias):
        return lax.dot_general(
            q, block, (((1,), (1,)), ((), ())), preferred_element_type=jnp.float32
        ) + bias[:, columns_of_bias]

    far_place, near_place, own_place = (slice(i * rows, (i + 1) * rows) for i in range(KV_STEPS))

    def finish_chunk(c):
        @pl.when(even & has_far_source)
        def _():
            for t in range(2):
                far(c, t).wait_recv()

        places = [
            pl.ds(pl.multiple_of((c * chunk_heads + h) * HEAD_DIM, HEAD_DIM), HEAD_DIM)
            for h in range(chunk_heads)
        ]
        first = []
        for place in places:
            q = q_own[:, place]
            s_far = scores(q, k_buf[0, :, place], far_place)
            s_own = scores(q, k_own[:, place], own_place)
            m = jnp.maximum(jnp.max(s_far, axis=1, keepdims=True), jnp.max(s_own, axis=1, keepdims=True))
            w_far = jnp.exp2((s_far - m) * factor)
            w_own = jnp.exp2((s_own - m) * factor)
            total = jnp.sum(w_far + w_own, axis=1, keepdims=True)
            mixed = jnp.dot(w_far.astype(jnp.bfloat16), v_buf[0, :, place], preferred_element_type=jnp.float32)
            mixed += jnp.dot(w_own.astype(jnp.bfloat16), v_own[:, place], preferred_element_type=jnp.float32)
            first.append((m, total, mixed))

        @pl.when(has_near_source)
        def _():
            near(c, 0).wait_recv()

        second = []
        for place, (m_first, total, mixed) in zip(places, first):
            s = scores(q_own[:, place], k_buf[1, :, place], near_place)
            m = jnp.maximum(m_first, jnp.max(s, axis=1, keepdims=True))
            w = jnp.exp2((s - m) * factor)
            scale = jnp.exp2((m_first - m) * factor)
            total = total * scale + jnp.sum(w, axis=1, keepdims=True)
            inverse = 1.0 / total
            second.append((w.astype(jnp.bfloat16), mixed * (scale * inverse), inverse))
            lse = m * (1.0 / math.sqrt(HEAD_DIM)) + jnp.log(total)
            diagonal = (lax.broadcasted_iota(jnp.int32, (rows, rows), 0)
                        == lax.broadcasted_iota(jnp.int32, (rows, rows), 1))
            lse_ref[pl.ds(c * chunk_heads + len(second) - 1, 1), :] = jnp.sum(
                jnp.where(diagonal, lse, 0.0), axis=0, keepdims=True)

        @pl.when(has_near_source)
        def _():
            near(c, 1).wait_recv()

        for place, (w, mixed, inverse) in zip(places, second):
            mixed += jnp.dot(w, v_buf[1, :, place], preferred_element_type=jnp.float32) * inverse
            o_ref[:, place] = mixed.astype(o_ref.dtype)

    def wait_far_sends(c):
        for t in range(2):
            far(c, t).wait_send()

    def wait_near_sends(c):
        for t in range(2):
            near(c, t).wait_send()

    def step(c):
        @pl.when(odd & has_far_source & (c < count))
        def _():
            for t in range(2):
                far(c, t).wait_recv()
                relay(c, t).start()

        @pl.when(odd & has_far_target & (c + ahead < count))
        def _():
            start_far(c + ahead)

        @pl.when(even & (c == count + LAG - 1))
        def _():
            each(0, count, wait_near_sends)

            @pl.when(has_far_target)
            def _():
                each(0, count, wait_far_sends)

        @pl.when(c >= LAG)
        def _():
            finish_chunk(c - LAG)

    each(0, count + LAG, step)

    @pl.when(odd & has_far_target)
    def _():
        each(0, count, wait_far_sends)

    @pl.when(odd & has_far_source)
    def _():
        each(0, count, wait_near_sends)


def write_kernel(o_vmem, lse_vmem, o_hbm, lse_hbm, sem):
    copies = [
        pltpu.make_async_copy(o_vmem, o_hbm, sem.at[0]),
        pltpu.make_async_copy(lse_vmem, lse_hbm, sem.at[1]),
    ]
    for copy in copies:
        copy.start()
    for copy in copies:
        copy.wait()


def write(attn_out, attn_lse):
    return pl.pallas_call(
        write_kernel,
        out_shape=(
            jax.ShapeDtypeStruct(attn_out.shape, attn_out.dtype),
            jax.ShapeDtypeStruct(attn_lse.shape, attn_lse.dtype),
        ),
        in_specs=[pl.BlockSpec(memory_space=pltpu.VMEM)] * 2,
        out_specs=(pl.BlockSpec(memory_space=pltpu.HBM),) * 2,
        scratch_shapes=[pltpu.SemaphoreType.DMA((2,))],
        compiler_params=pltpu.CompilerParams(vmem_limit_bytes=32 * 1024 * 1024),
        cost_estimate=pl.CostEstimate(
            flops=0, bytes_accessed=4 * attn_out.size, transcendentals=0),
    )(*(pltpu.with_memory_space_constraint(x, pltpu.VMEM) for x in (attn_out, attn_lse)))


def shards(n, att_query, att_key, att_value):
    rows, total_width = att_query.shape
    heads = total_width // HEAD_DIM
    chunk_heads = math.gcd(heads, CHUNK_HEADS)
    count = heads // chunk_heads
    bf16 = att_query.dtype
    attn_out, attn_lse = pl.pallas_call(
        functools.partial(kernel, n, chunk_heads),
        out_shape=(
            pltpu.VMEM((rows, total_width), bf16),
            pltpu.VMEM((heads, rows), jnp.float32),
        ),
        in_specs=[pl.BlockSpec(memory_space=pltpu.HBM)] * 3,
        out_specs=(pl.BlockSpec(memory_space=pltpu.VMEM), pl.BlockSpec(memory_space=pltpu.VMEM)),
        scratch_shapes=[
            pltpu.VMEM((rows, total_width), bf16),
            pltpu.VMEM((rows, total_width), bf16),
            pltpu.VMEM((rows, total_width), bf16),
            pltpu.VMEM((KV_STEPS - 1, rows, total_width), bf16),
            pltpu.VMEM((KV_STEPS - 1, rows, total_width), bf16),
            pltpu.VMEM((rows, KV_STEPS * rows), jnp.float32),
            pltpu.SemaphoreType.DMA((3,)),
            pltpu.SemaphoreType.DMA((count, 2)),
            pltpu.SemaphoreType.DMA((count, 2)),
            pltpu.SemaphoreType.DMA((count, 2)),
            pltpu.SemaphoreType.DMA((count, 2)),
        ],
        compiler_params=pltpu.CompilerParams(
            collective_id=0, has_side_effects=True, vmem_limit_bytes=32 * 1024 * 1024),
        cost_estimate=pl.CostEstimate(
            flops=4 * rows * rows * KV_STEPS * total_width,
            bytes_accessed=8 * rows * total_width,
            transcendentals=rows * rows * KV_STEPS * heads),
    )(*(pltpu.with_memory_space_constraint(x, pltpu.HBM) for x in (att_query, att_key, att_value)))
    return write(attn_out, attn_lse)


def solution(mesh):
    spec = P(("dp", "ctx"), None)
    return jax.shard_map(
        functools.partial(shards, mesh.shape["ctx"]),
        mesh=mesh,
        in_specs=(spec, spec, spec),
        out_specs=(spec, P(None, ("dp", "ctx"))),
        check_vma=False,
    )
```

```python
import functools
import math

import jax
import jax.numpy as jnp
from jax import lax
from jax.experimental import pallas as pl
from jax.experimental.pallas import tpu as pltpu
from jax.sharding import PartitionSpec as P

HEAD_DIM = 128
KV_STEPS = 3
CHUNK_HEADS = 2
AHEAD_ODD = 3
LAG = 1
MESH = pl.DeviceIdType.MESH


def kernel(
    n, q_hbm, k_hbm, v_hbm, o_ref, lse_ref,
    q_own, k_own, v_own, k_buf, v_buf, bias,
    in_sem, far_send, far_recv, near_send, near_recv,
):
    count, rows, width = k_own.shape
    chunk_heads = width // HEAD_DIM
    ahead = min(AHEAD_ODD, count)
    me = lax.axis_index("ctx")
    odd = lax.rem(me, 2) == 1
    even = jnp.logical_not(odd)
    partner = me + 1 - 2 * lax.rem(me, 2)
    has_far_target = me + 2 < n
    has_far_source = me >= 2
    has_near_source = me >= 1
    own = (k_own, v_own)
    bufs = (k_buf, v_buf)

    def columns(c):
        return pl.ds(pl.multiple_of(c * width, width), width)

    def far(c, t):
        return pltpu.make_async_remote_copy(
            src_ref=own[t].at[c], dst_ref=bufs[t].at[0, c],
            send_sem=far_send.at[c, t], recv_sem=far_recv.at[c, t],
            device_id={"ctx": lax.rem(me + 2, n)}, device_id_type=MESH)

    def near(c, t):
        return pltpu.make_async_remote_copy(
            src_ref=own[t].at[c], dst_ref=bufs[t].at[1, c],
            send_sem=near_send.at[c, t], recv_sem=near_recv.at[c, t],
            device_id={"ctx": partner}, device_id_type=MESH)

    def relay(c, t):
        return pltpu.make_async_remote_copy(
            src_ref=bufs[t].at[0, c], dst_ref=bufs[t].at[1, c],
            send_sem=near_send.at[c, t], recv_sem=near_recv.at[c, t],
            device_id={"ctx": partner}, device_id_type=MESH)

    def local(c, t):
        source = (k_hbm, v_hbm, q_hbm)[t]
        target = (k_own, v_own, q_own)[t]
        return pltpu.make_async_copy(source.at[:, columns(c)], target.at[c], in_sem.at[c, t])

    def each(start, stop, body):
        def step(c, carry):
            body(c)
            return carry
        lax.fori_loop(start, stop, step, 0)

    barrier = pltpu.get_barrier_semaphore()
    pl.semaphore_signal(barrier, inc=1, device_id={"ctx": partner}, device_id_type=MESH)

    @pl.when(has_far_target)
    def _():
        pl.semaphore_signal(barrier, inc=1, device_id={"ctx": lax.rem(me + 2, n)}, device_id_type=MESH)

    @pl.when(has_far_source)
    def _():
        pl.semaphore_signal(barrier, inc=1, device_id={"ctx": lax.rem(me + n - 2, n)}, device_id_type=MESH)

    def start_local(c):
        for t in range(2):
            local(c, t).start()

    each(0, count, start_local)

    pl.semaphore_wait(barrier, 1 + has_far_target.astype(jnp.int32) + has_far_source.astype(jnp.int32))

    def start_far(c):
        for t in range(2):
            far(c, t).start()

    def start_near(c):
        for t in range(2):
            near(c, t).start()

    def wait_local(c):
        for t in range(2):
            local(c, t).wait()

    def first_sends(c):
        wait_local(c)

        @pl.when(even)
        def _():
            start_near(c)

        @pl.when(has_far_target & (even | (c < ahead)))
        def _():
            start_far(c)

    each(0, count, first_sends)
    each(0, count, lambda c: local(c, 2).start())

    @pl.when(jnp.logical_not(has_far_source))
    def _():
        k_buf[0] = jnp.zeros(k_buf.shape[1:], k_buf.dtype)
        v_buf[0] = jnp.zeros(v_buf.shape[1:], v_buf.dtype)

    @pl.when(jnp.logical_not(has_near_source))
    def _():
        k_buf[1] = jnp.zeros(k_buf.shape[1:], k_buf.dtype)
        v_buf[1] = jnp.zeros(v_buf.shape[1:], v_buf.dtype)

    query = lax.broadcasted_iota(jnp.int32, (rows, KV_STEPS * rows), 0)
    key = lax.broadcasted_iota(jnp.int32, (rows, KV_STEPS * rows), 1)
    back = KV_STEPS - 1 - key // rows
    allowed = (back <= me) & ((back > 0) | (key - (KV_STEPS - 1) * rows <= query))
    bias[...] = jnp.where(allowed, 0.0, -jnp.inf)
    factor = math.log2(math.e) / math.sqrt(HEAD_DIM)

    each(0, count, lambda c: local(c, 2).wait())

    def scores(q, block, columns_of_bias):
        return lax.dot_general(
            q, block, (((1,), (1,)), ((), ())), preferred_element_type=jnp.float32
        ) + bias[:, columns_of_bias]

    far_place, near_place, own_place = (slice(i * rows, (i + 1) * rows) for i in range(KV_STEPS))

    def finish_chunk(c):
        @pl.when(even & has_far_source)
        def _():
            for t in range(2):
                far(c, t).wait_recv()

        places = [slice(h * HEAD_DIM, (h + 1) * HEAD_DIM) for h in range(chunk_heads)]
        first = []
        for place in places:
            q = q_own[c, :, place]
            s_far = scores(q, k_buf[0, c, :, place], far_place)
            s_own = scores(q, k_own[c, :, place], own_place)
            m = jnp.maximum(jnp.max(s_far, axis=1, keepdims=True), jnp.max(s_own, axis=1, keepdims=True))
            w_far = jnp.exp2((s_far - m) * factor)
            w_own = jnp.exp2((s_own - m) * factor)
            total = jnp.sum(w_far + w_own, axis=1, keepdims=True)
            mixed = jnp.dot(w_far.astype(jnp.bfloat16), v_buf[0, c, :, place], preferred_element_type=jnp.float32)
            mixed += jnp.dot(w_own.astype(jnp.bfloat16), v_own[c, :, place], preferred_element_type=jnp.float32)
            first.append((m, total, mixed))

        @pl.when(has_near_source)
        def _():
            near(c, 0).wait_recv()

        second = []
        for place, (m_first, total, mixed) in zip(places, first):
            s = scores(q_own[c, :, place], k_buf[1, c, :, place], near_place)
            m = jnp.maximum(m_first, jnp.max(s, axis=1, keepdims=True))
            w = jnp.exp2((s - m) * factor)
            scale = jnp.exp2((m_first - m) * factor)
            total = total * scale + jnp.sum(w, axis=1, keepdims=True)
            inverse = 1.0 / total
            second.append((w.astype(jnp.bfloat16), mixed * (scale * inverse), inverse))
            lse = m * (1.0 / math.sqrt(HEAD_DIM)) + jnp.log(total)
            diagonal = (lax.broadcasted_iota(jnp.int32, (rows, rows), 0)
                        == lax.broadcasted_iota(jnp.int32, (rows, rows), 1))
            lse_ref[pl.ds(c * chunk_heads + len(second) - 1, 1), :] = jnp.sum(
                jnp.where(diagonal, lse, 0.0), axis=0, keepdims=True)

        @pl.when(has_near_source)
        def _():
            near(c, 1).wait_recv()

        for h, (w, mixed, inverse) in enumerate(second):
            mixed += jnp.dot(w, v_buf[1, c, :, places[h]], preferred_element_type=jnp.float32) * inverse
            place = pl.ds(pl.multiple_of((c * chunk_heads + h) * HEAD_DIM, HEAD_DIM), HEAD_DIM)
            o_ref[:, place] = mixed.astype(o_ref.dtype)

    def wait_far_sends(c):
        for t in range(2):
            far(c, t).wait_send()

    def wait_near_sends(c):
        for t in range(2):
            near(c, t).wait_send()

    def step(c):
        @pl.when(odd & has_far_source & (c < count))
        def _():
            for t in range(2):
                far(c, t).wait_recv()
                relay(c, t).start()

        @pl.when(odd & has_far_target & (c + ahead < count))
        def _():
            start_far(c + ahead)

        @pl.when(c == count + LAG - 1)
        def _():
            @pl.when(has_far_target)
            def _():
                each(0, count, wait_far_sends)

            @pl.when(even | has_far_source)
            def _():
                each(0, count - 2, wait_near_sends)

        @pl.when(c >= LAG)
        def _():
            finish_chunk(c - LAG)

    each(0, count + LAG, step)

    @pl.when(even | has_far_source)
    def _():
        each(count - 2, count, wait_near_sends)


def write_kernel(o_vmem, lse_vmem, o_hbm, lse_hbm, sem):
    copies = [
        pltpu.make_async_copy(o_vmem, o_hbm, sem.at[0]),
        pltpu.make_async_copy(lse_vmem, lse_hbm, sem.at[1]),
    ]
    for copy in copies:
        copy.start()
    for copy in copies:
        copy.wait()


def write(attn_out, attn_lse):
    return pl.pallas_call(
        write_kernel,
        out_shape=(
            jax.ShapeDtypeStruct(attn_out.shape, attn_out.dtype),
            jax.ShapeDtypeStruct(attn_lse.shape, attn_lse.dtype),
        ),
        in_specs=[pl.BlockSpec(memory_space=pltpu.VMEM)] * 2,
        out_specs=(pl.BlockSpec(memory_space=pltpu.HBM),) * 2,
        scratch_shapes=[pltpu.SemaphoreType.DMA((2,))],
        compiler_params=pltpu.CompilerParams(vmem_limit_bytes=32 * 1024 * 1024),
        cost_estimate=pl.CostEstimate(
            flops=0, bytes_accessed=4 * attn_out.size, transcendentals=0),
    )(*(pltpu.with_memory_space_constraint(x, pltpu.VMEM) for x in (attn_out, attn_lse)))


def shards(n, att_query, att_key, att_value):
    rows, total_width = att_query.shape
    heads = total_width // HEAD_DIM
    chunk_heads = math.gcd(heads, CHUNK_HEADS)
    count = heads // chunk_heads
    width = chunk_heads * HEAD_DIM
    bf16 = att_query.dtype
    attn_out, attn_lse = pl.pallas_call(
        functools.partial(kernel, n),
        out_shape=(
            pltpu.VMEM((rows, total_width), bf16),
            pltpu.VMEM((heads, rows), jnp.float32),
        ),
        in_specs=[pl.BlockSpec(memory_space=pltpu.HBM)] * 3,
        out_specs=(pl.BlockSpec(memory_space=pltpu.VMEM), pl.BlockSpec(memory_space=pltpu.VMEM)),
        scratch_shapes=[
            pltpu.VMEM((count, rows, width), bf16),
            pltpu.VMEM((count, rows, width), bf16),
            pltpu.VMEM((count, rows, width), bf16),
            pltpu.VMEM((KV_STEPS - 1, count, rows, width), bf16),
            pltpu.VMEM((KV_STEPS - 1, count, rows, width), bf16),
            pltpu.VMEM((rows, KV_STEPS * rows), jnp.float32),
            pltpu.SemaphoreType.DMA((count, 3)),
            pltpu.SemaphoreType.DMA((count, 2)),
            pltpu.SemaphoreType.DMA((count, 2)),
            pltpu.SemaphoreType.DMA((count, 2)),
            pltpu.SemaphoreType.DMA((count, 2)),
        ],
        compiler_params=pltpu.CompilerParams(
            collective_id=0, has_side_effects=True, vmem_limit_bytes=32 * 1024 * 1024),
        cost_estimate=pl.CostEstimate(
            flops=4 * rows * rows * KV_STEPS * total_width,
            bytes_accessed=8 * rows * total_width,
            transcendentals=rows * rows * KV_STEPS * heads),
    )(*(pltpu.with_memory_space_constraint(x, pltpu.HBM) for x in (att_query, att_key, att_value)))
    return write(attn_out, attn_lse)


def solution(mesh):
    spec = P(("dp", "ctx"), None)
    return jax.shard_map(
        functools.partial(shards, mesh.shape["ctx"]),
        mesh=mesh,
        in_specs=(spec, spec, spec),
        out_specs=(spec, P(None, ("dp", "ctx"))),
        check_vma=False,
    )
```

```python
import functools
import math

import jax
import jax.numpy as jnp
from jax import lax
from jax.experimental import pallas as pl
from jax.experimental.pallas import tpu as pltpu
from jax.sharding import PartitionSpec as P

HEAD_DIM = 128
KV_STEPS = 3
CHUNK_HEADS = 2
AHEAD_ODD = 3
LAG = 1
MESH = pl.DeviceIdType.MESH


def kernel(
    n, q_hbm, k_hbm, v_hbm, o_ref, lse_ref,
    q_own, k_own, v_own, k_buf, v_buf, bias,
    in_sem, far_send, far_recv, near_send, near_recv, direct_send,
):
    count, rows, width = k_own.shape
    chunk_heads = width // HEAD_DIM
    ahead = min(AHEAD_ODD, count)
    me = lax.axis_index("ctx")
    odd = lax.rem(me, 2) == 1
    even = jnp.logical_not(odd)
    partner = me + 1 - 2 * lax.rem(me, 2)
    has_far_target = me + 2 < n
    has_far_source = me >= 2
    has_near_source = me >= 1
    has_direct_target = odd & (me + 1 < n)
    has_direct_source = even & (me >= 1)
    own = (k_own, v_own)
    bufs = (k_buf, v_buf)

    def columns(c):
        return pl.ds(pl.multiple_of(c * width, width), width)

    def far(c, t):
        return pltpu.make_async_remote_copy(
            src_ref=own[t].at[c], dst_ref=bufs[t].at[0, c],
            send_sem=far_send.at[c, t], recv_sem=far_recv.at[c, t],
            device_id={"ctx": lax.rem(me + 2, n)}, device_id_type=MESH)

    def near(c, t):
        return pltpu.make_async_remote_copy(
            src_ref=own[t].at[c], dst_ref=bufs[t].at[1, c],
            send_sem=near_send.at[c, t], recv_sem=near_recv.at[c, t],
            device_id={"ctx": partner}, device_id_type=MESH)

    def relay(c, t):
        return pltpu.make_async_remote_copy(
            src_ref=bufs[t].at[0, c], dst_ref=bufs[t].at[1, c],
            send_sem=near_send.at[c, t], recv_sem=near_recv.at[c, t],
            device_id={"ctx": partner}, device_id_type=MESH)

    def direct():
        return pltpu.make_async_remote_copy(
            src_ref=own[0].at[0], dst_ref=bufs[0].at[1, 0],
            send_sem=direct_send.at[0], recv_sem=near_recv.at[0, 0],
            device_id={"ctx": lax.rem(me + 1, n)}, device_id_type=MESH)

    def local(c, t):
        source = (k_hbm, v_hbm, q_hbm)[t]
        target = (k_own, v_own, q_own)[t]
        return pltpu.make_async_copy(source.at[:, columns(c)], target.at[c], in_sem.at[c, t])

    def each(start, stop, body):
        def step(c, carry):
            body(c)
            return carry
        lax.fori_loop(start, stop, step, 0)

    barrier = pltpu.get_barrier_semaphore()
    pl.semaphore_signal(barrier, inc=1, device_id={"ctx": partner}, device_id_type=MESH)

    @pl.when(has_far_target)
    def _():
        pl.semaphore_signal(barrier, inc=1, device_id={"ctx": lax.rem(me + 2, n)}, device_id_type=MESH)

    @pl.when(has_far_source)
    def _():
        pl.semaphore_signal(barrier, inc=1, device_id={"ctx": lax.rem(me + n - 2, n)}, device_id_type=MESH)

    @pl.when(has_direct_target)
    def _():
        pl.semaphore_signal(barrier, inc=1, device_id={"ctx": lax.rem(me + 1, n)}, device_id_type=MESH)

    @pl.when(has_direct_source)
    def _():
        pl.semaphore_signal(barrier, inc=1, device_id={"ctx": lax.rem(me + n - 1, n)}, device_id_type=MESH)

    def start_local(c):
        for t in range(2):
            local(c, t).start()

    each(0, count, start_local)

    peers = (has_far_target, has_far_source, has_direct_target, has_direct_source)
    pl.semaphore_wait(barrier, 1 + sum(peer.astype(jnp.int32) for peer in peers))

    def start_far(c):
        for t in range(2):
            far(c, t).start()

    def start_near(c):
        for t in range(2):
            near(c, t).start()

    def wait_local(c):
        for t in range(2):
            local(c, t).wait()

    def first_sends(c):
        wait_local(c)

        @pl.when(even)
        def _():
            start_near(c)

        @pl.when(has_far_target & (even | (c < ahead)))
        def _():
            start_far(c)

        @pl.when(has_direct_target & (c == 0))
        def _():
            direct().start()

    each(0, count, first_sends)
    each(0, count, lambda c: local(c, 2).start())

    @pl.when(jnp.logical_not(has_far_source))
    def _():
        k_buf[0] = jnp.zeros(k_buf.shape[1:], k_buf.dtype)
        v_buf[0] = jnp.zeros(v_buf.shape[1:], v_buf.dtype)

    @pl.when(jnp.logical_not(has_near_source))
    def _():
        k_buf[1] = jnp.zeros(k_buf.shape[1:], k_buf.dtype)
        v_buf[1] = jnp.zeros(v_buf.shape[1:], v_buf.dtype)

    query = lax.broadcasted_iota(jnp.int32, (rows, KV_STEPS * rows), 0)
    key = lax.broadcasted_iota(jnp.int32, (rows, KV_STEPS * rows), 1)
    back = KV_STEPS - 1 - key // rows
    allowed = (back <= me) & ((back > 0) | (key - (KV_STEPS - 1) * rows <= query))
    bias[...] = jnp.where(allowed, 0.0, -jnp.inf)
    factor = math.log2(math.e) / math.sqrt(HEAD_DIM)

    each(0, count, lambda c: local(c, 2).wait())

    def scores(q, block, columns_of_bias):
        return lax.dot_general(
            q, block, (((1,), (1,)), ((), ())), preferred_element_type=jnp.float32
        ) + bias[:, columns_of_bias]

    far_place, near_place, own_place = (slice(i * rows, (i + 1) * rows) for i in range(KV_STEPS))

    def finish_chunk(c):
        @pl.when(even & has_far_source)
        def _():
            for t in range(2):
                far(c, t).wait_recv()

        places = [slice(h * HEAD_DIM, (h + 1) * HEAD_DIM) for h in range(chunk_heads)]
        first = []
        for place in places:
            q = q_own[c, :, place]
            s_far = scores(q, k_buf[0, c, :, place], far_place)
            s_own = scores(q, k_own[c, :, place], own_place)
            m = jnp.maximum(jnp.max(s_far, axis=1, keepdims=True), jnp.max(s_own, axis=1, keepdims=True))
            w_far = jnp.exp2((s_far - m) * factor)
            w_own = jnp.exp2((s_own - m) * factor)
            total = jnp.sum(w_far + w_own, axis=1, keepdims=True)
            mixed = jnp.dot(w_far.astype(jnp.bfloat16), v_buf[0, c, :, place], preferred_element_type=jnp.float32)
            mixed += jnp.dot(w_own.astype(jnp.bfloat16), v_own[c, :, place], preferred_element_type=jnp.float32)
            first.append((m, total, mixed))

        @pl.when(has_near_source)
        def _():
            near(c, 0).wait_recv()

        second = []
        for place, (m_first, total, mixed) in zip(places, first):
            s = scores(q_own[c, :, place], k_buf[1, c, :, place], near_place)
            m = jnp.maximum(m_first, jnp.max(s, axis=1, keepdims=True))
            w = jnp.exp2((s - m) * factor)
            scale = jnp.exp2((m_first - m) * factor)
            total = total * scale + jnp.sum(w, axis=1, keepdims=True)
            inverse = 1.0 / total
            second.append((w.astype(jnp.bfloat16), mixed * (scale * inverse), inverse))
            lse = m * (1.0 / math.sqrt(HEAD_DIM)) + jnp.log(total)
            diagonal = (lax.broadcasted_iota(jnp.int32, (rows, rows), 0)
                        == lax.broadcasted_iota(jnp.int32, (rows, rows), 1))
            lse_ref[pl.ds(c * chunk_heads + len(second) - 1, 1), :] = jnp.sum(
                jnp.where(diagonal, lse, 0.0), axis=0, keepdims=True)

        @pl.when(has_near_source)
        def _():
            near(c, 1).wait_recv()

        for h, (w, mixed, inverse) in enumerate(second):
            mixed += jnp.dot(w, v_buf[1, c, :, places[h]], preferred_element_type=jnp.float32) * inverse
            place = pl.ds(pl.multiple_of((c * chunk_heads + h) * HEAD_DIM, HEAD_DIM), HEAD_DIM)
            o_ref[:, place] = mixed.astype(o_ref.dtype)

    def wait_far_sends(c):
        for t in range(2):
            far(c, t).wait_send()

    def wait_near_sends(c):
        @pl.when(even | (c > 0))
        def _():
            near(c, 0).wait_send()

        near(c, 1).wait_send()

    def step(c):
        @pl.when(odd & has_far_source & (c < count))
        def _():
            far(c, 0).wait_recv()

            @pl.when(c > 0)
            def _():
                relay(c, 0).start()

            far(c, 1).wait_recv()
            relay(c, 1).start()

        @pl.when(odd & has_far_target & (c + ahead < count))
        def _():
            start_far(c + ahead)

        @pl.when(c == count + LAG - 1)
        def _():
            @pl.when(has_far_target)
            def _():
                each(0, count, wait_far_sends)

            @pl.when(even | has_far_source)
            def _():
                each(0, count - 2, wait_near_sends)

        @pl.when(c >= LAG)
        def _():
            finish_chunk(c - LAG)

    each(0, count + LAG, step)

    @pl.when(even | has_far_source)
    def _():
        each(count - 2, count, wait_near_sends)

    @pl.when(has_direct_target)
    def _():
        direct().wait_send()


def write_kernel(o_vmem, lse_vmem, o_hbm, lse_hbm, sem):
    copies = [
        pltpu.make_async_copy(o_vmem, o_hbm, sem.at[0]),
        pltpu.make_async_copy(lse_vmem, lse_hbm, sem.at[1]),
    ]
    for copy in copies:
        copy.start()
    for copy in copies:
        copy.wait()


def write(attn_out, attn_lse):
    return pl.pallas_call(
        write_kernel,
        out_shape=(
            jax.ShapeDtypeStruct(attn_out.shape, attn_out.dtype),
            jax.ShapeDtypeStruct(attn_lse.shape, attn_lse.dtype),
        ),
        in_specs=[pl.BlockSpec(memory_space=pltpu.VMEM)] * 2,
        out_specs=(pl.BlockSpec(memory_space=pltpu.HBM),) * 2,
        scratch_shapes=[pltpu.SemaphoreType.DMA((2,))],
        compiler_params=pltpu.CompilerParams(vmem_limit_bytes=32 * 1024 * 1024),
        cost_estimate=pl.CostEstimate(
            flops=0, bytes_accessed=4 * attn_out.size, transcendentals=0),
    )(*(pltpu.with_memory_space_constraint(x, pltpu.VMEM) for x in (attn_out, attn_lse)))


def shards(n, att_query, att_key, att_value):
    rows, total_width = att_query.shape
    heads = total_width // HEAD_DIM
    chunk_heads = math.gcd(heads, CHUNK_HEADS)
    count = heads // chunk_heads
    width = chunk_heads * HEAD_DIM
    bf16 = att_query.dtype
    attn_out, attn_lse = pl.pallas_call(
        functools.partial(kernel, n),
        out_shape=(
            pltpu.VMEM((rows, total_width), bf16),
            pltpu.VMEM((heads, rows), jnp.float32),
        ),
        in_specs=[pl.BlockSpec(memory_space=pltpu.HBM)] * 3,
        out_specs=(pl.BlockSpec(memory_space=pltpu.VMEM), pl.BlockSpec(memory_space=pltpu.VMEM)),
        scratch_shapes=[
            pltpu.VMEM((count, rows, width), bf16),
            pltpu.VMEM((count, rows, width), bf16),
            pltpu.VMEM((count, rows, width), bf16),
            pltpu.VMEM((KV_STEPS - 1, count, rows, width), bf16),
            pltpu.VMEM((KV_STEPS - 1, count, rows, width), bf16),
            pltpu.VMEM((rows, KV_STEPS * rows), jnp.float32),
            pltpu.SemaphoreType.DMA((count, 3)),
            pltpu.SemaphoreType.DMA((count, 2)),
            pltpu.SemaphoreType.DMA((count, 2)),
            pltpu.SemaphoreType.DMA((count, 2)),
            pltpu.SemaphoreType.DMA((count, 2)),
            pltpu.SemaphoreType.DMA((1,)),
        ],
        compiler_params=pltpu.CompilerParams(
            collective_id=0, has_side_effects=True, vmem_limit_bytes=32 * 1024 * 1024),
        cost_estimate=pl.CostEstimate(
            flops=4 * rows * rows * KV_STEPS * total_width,
            bytes_accessed=8 * rows * total_width,
            transcendentals=rows * rows * KV_STEPS * heads),
    )(*(pltpu.with_memory_space_constraint(x, pltpu.HBM) for x in (att_query, att_key, att_value)))
    return write(attn_out, attn_lse)


def solution(mesh):
    spec = P(("dp", "ctx"), None)
    return jax.shard_map(
        functools.partial(shards, mesh.shape["ctx"]),
        mesh=mesh,
        in_specs=(spec, spec, spec),
        out_specs=(spec, P(None, ("dp", "ctx"))),
        check_vma=False,
    )
```

```python
import functools
import math

import jax
import jax.numpy as jnp
from jax import lax
from jax.experimental import pallas as pl
from jax.experimental.pallas import tpu as pltpu
from jax.sharding import PartitionSpec as P

HEAD_DIM = 128
KV_STEPS = 3
CHUNK_HEADS = 1
AHEAD_ODD = 5
LAG = 1
MESH = pl.DeviceIdType.MESH


def kernel(
    n, q_hbm, k_hbm, v_hbm, o_ref, lse_ref,
    q_own, k_own, v_own, k_buf, v_buf, bias,
    in_sem, far_send, far_recv, near_send, near_recv,
):
    count, rows, width = k_own.shape
    chunk_heads = width // HEAD_DIM
    ahead = min(AHEAD_ODD, count)
    me = lax.axis_index("ctx")
    odd = lax.rem(me, 2) == 1
    even = jnp.logical_not(odd)
    partner = me + 1 - 2 * lax.rem(me, 2)
    has_far_target = me + 2 < n
    has_far_source = me >= 2
    has_near_source = me >= 1
    own = (k_own, v_own)
    bufs = (k_buf, v_buf)

    def columns(c):
        return pl.ds(pl.multiple_of(c * width, width), width)

    def far(c, t):
        return pltpu.make_async_remote_copy(
            src_ref=own[t].at[c], dst_ref=bufs[t].at[0, c],
            send_sem=far_send.at[c, t], recv_sem=far_recv.at[c, t],
            device_id={"ctx": lax.rem(me + 2, n)}, device_id_type=MESH)

    def near(c, t):
        return pltpu.make_async_remote_copy(
            src_ref=own[t].at[c], dst_ref=bufs[t].at[1, c],
            send_sem=near_send.at[c, t], recv_sem=near_recv.at[c, t],
            device_id={"ctx": partner}, device_id_type=MESH)

    def relay(c, t):
        return pltpu.make_async_remote_copy(
            src_ref=bufs[t].at[0, c], dst_ref=bufs[t].at[1, c],
            send_sem=near_send.at[c, t], recv_sem=near_recv.at[c, t],
            device_id={"ctx": partner}, device_id_type=MESH)

    def local(c, t):
        source = (k_hbm, v_hbm, q_hbm)[t]
        target = (k_own, v_own, q_own)[t]
        return pltpu.make_async_copy(source.at[:, columns(c)], target.at[c], in_sem.at[c, t])

    def each(start, stop, body):
        def step(c, carry):
            body(c)
            return carry
        lax.fori_loop(start, stop, step, 0)

    barrier = pltpu.get_barrier_semaphore()
    pl.semaphore_signal(barrier, inc=1, device_id={"ctx": partner}, device_id_type=MESH)

    @pl.when(has_far_target)
    def _():
        pl.semaphore_signal(barrier, inc=1, device_id={"ctx": lax.rem(me + 2, n)}, device_id_type=MESH)

    @pl.when(has_far_source)
    def _():
        pl.semaphore_signal(barrier, inc=1, device_id={"ctx": lax.rem(me + n - 2, n)}, device_id_type=MESH)

    def start_local(c):
        for t in range(2):
            local(c, t).start()

    each(0, count, start_local)

    pl.semaphore_wait(barrier, 1 + has_far_target.astype(jnp.int32) + has_far_source.astype(jnp.int32))

    def start_far(c):
        for t in range(2):
            far(c, t).start()

    def start_near(c):
        for t in range(2):
            near(c, t).start()

    def wait_local(c):
        for t in range(2):
            local(c, t).wait()

    def first_sends(c):
        wait_local(c)

        @pl.when(even)
        def _():
            start_near(c)

        @pl.when(has_far_target & (even | (c < ahead)))
        def _():
            start_far(c)

    each(0, count, first_sends)
    each(0, count, lambda c: local(c, 2).start())

    @pl.when(jnp.logical_not(has_far_source))
    def _():
        k_buf[0] = jnp.zeros(k_buf.shape[1:], k_buf.dtype)
        v_buf[0] = jnp.zeros(v_buf.shape[1:], v_buf.dtype)

    @pl.when(jnp.logical_not(has_near_source))
    def _():
        k_buf[1] = jnp.zeros(k_buf.shape[1:], k_buf.dtype)
        v_buf[1] = jnp.zeros(v_buf.shape[1:], v_buf.dtype)

    query = lax.broadcasted_iota(jnp.int32, (rows, KV_STEPS * rows), 0)
    key = lax.broadcasted_iota(jnp.int32, (rows, KV_STEPS * rows), 1)
    back = KV_STEPS - 1 - key // rows
    allowed = (back <= me) & ((back > 0) | (key - (KV_STEPS - 1) * rows <= query))
    bias[...] = jnp.where(allowed, 0.0, -jnp.inf)
    factor = math.log2(math.e) / math.sqrt(HEAD_DIM)

    each(0, count, lambda c: local(c, 2).wait())

    def scores(q, block, columns_of_bias):
        return lax.dot_general(
            q, block, (((1,), (1,)), ((), ())), preferred_element_type=jnp.float32
        ) + bias[:, columns_of_bias]

    far_place, near_place, own_place = (slice(i * rows, (i + 1) * rows) for i in range(KV_STEPS))

    def finish_chunk(c):
        @pl.when(even & has_far_source)
        def _():
            for t in range(2):
                far(c, t).wait_recv()

        places = [slice(h * HEAD_DIM, (h + 1) * HEAD_DIM) for h in range(chunk_heads)]
        first = []
        for place in places:
            q = q_own[c, :, place]
            s_far = scores(q, k_buf[0, c, :, place], far_place)
            s_own = scores(q, k_own[c, :, place], own_place)
            m = jnp.maximum(jnp.max(s_far, axis=1, keepdims=True), jnp.max(s_own, axis=1, keepdims=True))
            w_far = jnp.exp2((s_far - m) * factor)
            w_own = jnp.exp2((s_own - m) * factor)
            total = jnp.sum(w_far + w_own, axis=1, keepdims=True)
            mixed = jnp.dot(w_far.astype(jnp.bfloat16), v_buf[0, c, :, place], preferred_element_type=jnp.float32)
            mixed += jnp.dot(w_own.astype(jnp.bfloat16), v_own[c, :, place], preferred_element_type=jnp.float32)
            first.append((m, total, mixed))

        @pl.when(has_near_source)
        def _():
            near(c, 0).wait_recv()

        second = []
        for place, (m_first, total, mixed) in zip(places, first):
            s = scores(q_own[c, :, place], k_buf[1, c, :, place], near_place)
            m = jnp.maximum(m_first, jnp.max(s, axis=1, keepdims=True))
            w = jnp.exp2((s - m) * factor)
            scale = jnp.exp2((m_first - m) * factor)
            total = total * scale + jnp.sum(w, axis=1, keepdims=True)
            inverse = 1.0 / total
            second.append((w.astype(jnp.bfloat16), mixed * (scale * inverse), inverse))
            lse = m * (1.0 / math.sqrt(HEAD_DIM)) + jnp.log(total)
            diagonal = (lax.broadcasted_iota(jnp.int32, (rows, rows), 0)
                        == lax.broadcasted_iota(jnp.int32, (rows, rows), 1))
            lse_ref[pl.ds(c * chunk_heads + len(second) - 1, 1), :] = jnp.sum(
                jnp.where(diagonal, lse, 0.0), axis=0, keepdims=True)

        @pl.when(has_near_source)
        def _():
            near(c, 1).wait_recv()

        for h, (w, mixed, inverse) in enumerate(second):
            mixed += jnp.dot(w, v_buf[1, c, :, places[h]], preferred_element_type=jnp.float32) * inverse
            place = pl.ds(pl.multiple_of((c * chunk_heads + h) * HEAD_DIM, HEAD_DIM), HEAD_DIM)
            o_ref[:, place] = mixed.astype(o_ref.dtype)

    def wait_far_sends(c):
        for t in range(2):
            far(c, t).wait_send()

    def wait_near_sends(c):
        for t in range(2):
            near(c, t).wait_send()

    def step(c):
        @pl.when(odd & has_far_source & (c < count))
        def _():
            for t in range(2):
                far(c, t).wait_recv()
                relay(c, t).start()

        @pl.when(odd & has_far_target & (c + ahead < count))
        def _():
            start_far(c + ahead)

        @pl.when(c == count + LAG - 1)
        def _():
            @pl.when(has_far_target)
            def _():
                each(0, count, wait_far_sends)

            @pl.when(even | has_far_source)
            def _():
                each(0, count - 2, wait_near_sends)

        @pl.when(c >= LAG)
        def _():
            finish_chunk(c - LAG)

    each(0, count + LAG, step)

    @pl.when(even | has_far_source)
    def _():
        each(count - 2, count, wait_near_sends)


def write_kernel(o_vmem, lse_vmem, o_hbm, lse_hbm, sem):
    copies = [
        pltpu.make_async_copy(o_vmem, o_hbm, sem.at[0]),
        pltpu.make_async_copy(lse_vmem, lse_hbm, sem.at[1]),
    ]
    for copy in copies:
        copy.start()
    for copy in copies:
        copy.wait()


def write(attn_out, attn_lse):
    return pl.pallas_call(
        write_kernel,
        out_shape=(
            jax.ShapeDtypeStruct(attn_out.shape, attn_out.dtype),
            jax.ShapeDtypeStruct(attn_lse.shape, attn_lse.dtype),
        ),
        in_specs=[pl.BlockSpec(memory_space=pltpu.VMEM)] * 2,
        out_specs=(pl.BlockSpec(memory_space=pltpu.HBM),) * 2,
        scratch_shapes=[pltpu.SemaphoreType.DMA((2,))],
        compiler_params=pltpu.CompilerParams(vmem_limit_bytes=32 * 1024 * 1024),
        cost_estimate=pl.CostEstimate(
            flops=0, bytes_accessed=4 * attn_out.size, transcendentals=0),
    )(*(pltpu.with_memory_space_constraint(x, pltpu.VMEM) for x in (attn_out, attn_lse)))


def shards(n, att_query, att_key, att_value):
    rows, total_width = att_query.shape
    heads = total_width // HEAD_DIM
    chunk_heads = math.gcd(heads, CHUNK_HEADS)
    count = heads // chunk_heads
    width = chunk_heads * HEAD_DIM
    bf16 = att_query.dtype
    attn_out, attn_lse = pl.pallas_call(
        functools.partial(kernel, n),
        out_shape=(
            pltpu.VMEM((rows, total_width), bf16),
            pltpu.VMEM((heads, rows), jnp.float32),
        ),
        in_specs=[pl.BlockSpec(memory_space=pltpu.HBM)] * 3,
        out_specs=(pl.BlockSpec(memory_space=pltpu.VMEM), pl.BlockSpec(memory_space=pltpu.VMEM)),
        scratch_shapes=[
            pltpu.VMEM((count, rows, width), bf16),
            pltpu.VMEM((count, rows, width), bf16),
            pltpu.VMEM((count, rows, width), bf16),
            pltpu.VMEM((KV_STEPS - 1, count, rows, width), bf16),
            pltpu.VMEM((KV_STEPS - 1, count, rows, width), bf16),
            pltpu.VMEM((rows, KV_STEPS * rows), jnp.float32),
            pltpu.SemaphoreType.DMA((count, 3)),
            pltpu.SemaphoreType.DMA((count, 2)),
            pltpu.SemaphoreType.DMA((count, 2)),
            pltpu.SemaphoreType.DMA((count, 2)),
            pltpu.SemaphoreType.DMA((count, 2)),
        ],
        compiler_params=pltpu.CompilerParams(
            collective_id=0, has_side_effects=True, vmem_limit_bytes=32 * 1024 * 1024),
        cost_estimate=pl.CostEstimate(
            flops=4 * rows * rows * KV_STEPS * total_width,
            bytes_accessed=8 * rows * total_width,
            transcendentals=rows * rows * KV_STEPS * heads),
    )(*(pltpu.with_memory_space_constraint(x, pltpu.HBM) for x in (att_query, att_key, att_value)))
    return write(attn_out, attn_lse)


def solution(mesh):
    spec = P(("dp", "ctx"), None)
    return jax.shard_map(
        functools.partial(shards, mesh.shape["ctx"]),
        mesh=mesh,
        in_specs=(spec, spec, spec),
        out_specs=(spec, P(None, ("dp", "ctx"))),
        check_vma=False,
    )
```

```python
import functools
import math

import jax
import jax.numpy as jnp
from jax import lax
from jax.experimental import pallas as pl
from jax.experimental.pallas import tpu as pltpu
from jax.sharding import PartitionSpec as P

HEAD_DIM = 128
KV_STEPS = 3
CHUNK_HEADS = 2
AHEAD_ODD = 3
LAG = 1
WRITES = 4
MESH = pl.DeviceIdType.MESH


def kernel(
    n, q_hbm, k_hbm, v_hbm, o_ref, lse_ref,
    q_own, k_own, v_own, k_buf, v_buf, bias,
    in_sem, far_send, far_recv, near_send, near_recv,
):
    count, rows, width = k_own.shape
    chunk_heads = width // HEAD_DIM
    ahead = min(AHEAD_ODD, count)
    me = lax.axis_index("ctx")
    odd = lax.rem(me, 2) == 1
    even = jnp.logical_not(odd)
    partner = me + 1 - 2 * lax.rem(me, 2)
    has_far_target = me + 2 < n
    has_far_source = me >= 2
    has_near_source = me >= 1
    own = (k_own, v_own)
    bufs = (k_buf, v_buf)

    def columns(c):
        return pl.ds(pl.multiple_of(c * width, width), width)

    def far(c, t):
        return pltpu.make_async_remote_copy(
            src_ref=own[t].at[c], dst_ref=bufs[t].at[0, c],
            send_sem=far_send.at[c, t], recv_sem=far_recv.at[c, t],
            device_id={"ctx": lax.rem(me + 2, n)}, device_id_type=MESH)

    def near(c, t):
        return pltpu.make_async_remote_copy(
            src_ref=own[t].at[c], dst_ref=bufs[t].at[1, c],
            send_sem=near_send.at[c, t], recv_sem=near_recv.at[c, t],
            device_id={"ctx": partner}, device_id_type=MESH)

    def relay(c, t):
        return pltpu.make_async_remote_copy(
            src_ref=bufs[t].at[0, c], dst_ref=bufs[t].at[1, c],
            send_sem=near_send.at[c, t], recv_sem=near_recv.at[c, t],
            device_id={"ctx": partner}, device_id_type=MESH)

    def local(c, t):
        source = (k_hbm, v_hbm, q_hbm)[t]
        target = (k_own, v_own, q_own)[t]
        return pltpu.make_async_copy(source.at[:, columns(c)], target.at[c], in_sem.at[c, t])

    def each(start, stop, body):
        def step(c, carry):
            body(c)
            return carry
        lax.fori_loop(start, stop, step, 0)

    barrier = pltpu.get_barrier_semaphore()
    pl.semaphore_signal(barrier, inc=1, device_id={"ctx": partner}, device_id_type=MESH)

    @pl.when(has_far_target)
    def _():
        pl.semaphore_signal(barrier, inc=1, device_id={"ctx": lax.rem(me + 2, n)}, device_id_type=MESH)

    @pl.when(has_far_source)
    def _():
        pl.semaphore_signal(barrier, inc=1, device_id={"ctx": lax.rem(me + n - 2, n)}, device_id_type=MESH)

    def start_local(c):
        for t in range(2):
            local(c, t).start()

    each(0, count, start_local)

    pl.semaphore_wait(barrier, 1 + has_far_target.astype(jnp.int32) + has_far_source.astype(jnp.int32))

    def start_far(c):
        for t in range(2):
            far(c, t).start()

    def start_near(c):
        for t in range(2):
            near(c, t).start()

    def wait_local(c):
        for t in range(2):
            local(c, t).wait()

    def first_sends(c):
        wait_local(c)

        @pl.when(even)
        def _():
            start_near(c)

        @pl.when(has_far_target & (even | (c < ahead)))
        def _():
            start_far(c)

    each(0, count, first_sends)
    each(0, count, lambda c: local(c, 2).start())

    @pl.when(jnp.logical_not(has_far_source))
    def _():
        k_buf[0] = jnp.zeros(k_buf.shape[1:], k_buf.dtype)
        v_buf[0] = jnp.zeros(v_buf.shape[1:], v_buf.dtype)

    @pl.when(jnp.logical_not(has_near_source))
    def _():
        k_buf[1] = jnp.zeros(k_buf.shape[1:], k_buf.dtype)
        v_buf[1] = jnp.zeros(v_buf.shape[1:], v_buf.dtype)

    query = lax.broadcasted_iota(jnp.int32, (rows, KV_STEPS * rows), 0)
    key = lax.broadcasted_iota(jnp.int32, (rows, KV_STEPS * rows), 1)
    back = KV_STEPS - 1 - key // rows
    allowed = (back <= me) & ((back > 0) | (key - (KV_STEPS - 1) * rows <= query))
    bias[...] = jnp.where(allowed, 0.0, -jnp.inf)
    factor = math.log2(math.e) / math.sqrt(HEAD_DIM)

    each(0, count, lambda c: local(c, 2).wait())

    def scores(q, block, columns_of_bias):
        return lax.dot_general(
            q, block, (((1,), (1,)), ((), ())), preferred_element_type=jnp.float32
        ) + bias[:, columns_of_bias]

    far_place, near_place, own_place = (slice(i * rows, (i + 1) * rows) for i in range(KV_STEPS))

    def finish_chunk(c):
        @pl.when(even & has_far_source)
        def _():
            for t in range(2):
                far(c, t).wait_recv()

        places = [slice(h * HEAD_DIM, (h + 1) * HEAD_DIM) for h in range(chunk_heads)]
        first = []
        for place in places:
            q = q_own[c, :, place]
            s_far = scores(q, k_buf[0, c, :, place], far_place)
            s_own = scores(q, k_own[c, :, place], own_place)
            m = jnp.maximum(jnp.max(s_far, axis=1, keepdims=True), jnp.max(s_own, axis=1, keepdims=True))
            w_far = jnp.exp2((s_far - m) * factor)
            w_own = jnp.exp2((s_own - m) * factor)
            total = jnp.sum(w_far + w_own, axis=1, keepdims=True)
            mixed = jnp.dot(w_far.astype(jnp.bfloat16), v_buf[0, c, :, place], preferred_element_type=jnp.float32)
            mixed += jnp.dot(w_own.astype(jnp.bfloat16), v_own[c, :, place], preferred_element_type=jnp.float32)
            first.append((m, total, mixed))

        @pl.when(has_near_source)
        def _():
            near(c, 0).wait_recv()

        second = []
        for place, (m_first, total, mixed) in zip(places, first):
            s = scores(q_own[c, :, place], k_buf[1, c, :, place], near_place)
            m = jnp.maximum(m_first, jnp.max(s, axis=1, keepdims=True))
            w = jnp.exp2((s - m) * factor)
            scale = jnp.exp2((m_first - m) * factor)
            total = total * scale + jnp.sum(w, axis=1, keepdims=True)
            inverse = 1.0 / total
            second.append((w.astype(jnp.bfloat16), mixed * (scale * inverse), inverse))
            lse = m * (1.0 / math.sqrt(HEAD_DIM)) + jnp.log(total)
            diagonal = (lax.broadcasted_iota(jnp.int32, (rows, rows), 0)
                        == lax.broadcasted_iota(jnp.int32, (rows, rows), 1))
            lse_ref[pl.ds(c * chunk_heads + len(second) - 1, 1), :] = jnp.sum(
                jnp.where(diagonal, lse, 0.0), axis=0, keepdims=True)

        @pl.when(has_near_source)
        def _():
            near(c, 1).wait_recv()

        for h, (w, mixed, inverse) in enumerate(second):
            mixed += jnp.dot(w, v_buf[1, c, :, places[h]], preferred_element_type=jnp.float32) * inverse
            place = pl.ds(pl.multiple_of((c * chunk_heads + h) * HEAD_DIM, HEAD_DIM), HEAD_DIM)
            o_ref[:, place] = mixed.astype(o_ref.dtype)

    def wait_far_sends(c):
        for t in range(2):
            far(c, t).wait_send()

    def wait_near_sends(c):
        for t in range(2):
            near(c, t).wait_send()

    def step(c):
        @pl.when(odd & has_far_source & (c < count))
        def _():
            for t in range(2):
                far(c, t).wait_recv()
                relay(c, t).start()

        @pl.when(odd & has_far_target & (c + ahead < count))
        def _():
            start_far(c + ahead)

        @pl.when(c == max(count + LAG - 2, 0))
        def _():
            @pl.when(has_far_target)
            def _():
                each(0, count, wait_far_sends)

            @pl.when(even | has_far_source)
            def _():
                each(0, count - 2, wait_near_sends)

        @pl.when(c >= LAG)
        def _():
            finish_chunk(c - LAG)

    each(0, count + LAG, step)

    @pl.when(even | has_far_source)
    def _():
        each(count - 2, count, wait_near_sends)


def write_kernel(o_vmem, lse_vmem, o_hbm, lse_hbm, sem):
    part = o_vmem.shape[0] // WRITES
    copies = [
        pltpu.make_async_copy(
            o_vmem.at[pl.ds(i * part, part)], o_hbm.at[pl.ds(i * part, part)], sem.at[i])
        for i in range(WRITES)
    ] + [pltpu.make_async_copy(lse_vmem, lse_hbm, sem.at[WRITES])]
    for copy in copies:
        copy.start()
    for copy in copies:
        copy.wait()


def write(attn_out, attn_lse):
    return pl.pallas_call(
        write_kernel,
        out_shape=(
            jax.ShapeDtypeStruct(attn_out.shape, attn_out.dtype),
            jax.ShapeDtypeStruct(attn_lse.shape, attn_lse.dtype),
        ),
        in_specs=[pl.BlockSpec(memory_space=pltpu.VMEM)] * 2,
        out_specs=(pl.BlockSpec(memory_space=pltpu.HBM),) * 2,
        scratch_shapes=[pltpu.SemaphoreType.DMA((WRITES + 1,))],
        compiler_params=pltpu.CompilerParams(vmem_limit_bytes=32 * 1024 * 1024),
        cost_estimate=pl.CostEstimate(
            flops=0, bytes_accessed=4 * attn_out.size, transcendentals=0),
    )(*(pltpu.with_memory_space_constraint(x, pltpu.VMEM) for x in (attn_out, attn_lse)))


def shards(n, att_query, att_key, att_value):
    rows, total_width = att_query.shape
    heads = total_width // HEAD_DIM
    chunk_heads = math.gcd(heads, CHUNK_HEADS)
    count = heads // chunk_heads
    width = chunk_heads * HEAD_DIM
    bf16 = att_query.dtype
    attn_out, attn_lse = pl.pallas_call(
        functools.partial(kernel, n),
        out_shape=(
            pltpu.VMEM((rows, total_width), bf16),
            pltpu.VMEM((heads, rows), jnp.float32),
        ),
        in_specs=[pl.BlockSpec(memory_space=pltpu.HBM)] * 3,
        out_specs=(pl.BlockSpec(memory_space=pltpu.VMEM), pl.BlockSpec(memory_space=pltpu.VMEM)),
        scratch_shapes=[
            pltpu.VMEM((count, rows, width), bf16),
            pltpu.VMEM((count, rows, width), bf16),
            pltpu.VMEM((count, rows, width), bf16),
            pltpu.VMEM((KV_STEPS - 1, count, rows, width), bf16),
            pltpu.VMEM((KV_STEPS - 1, count, rows, width), bf16),
            pltpu.VMEM((rows, KV_STEPS * rows), jnp.float32),
            pltpu.SemaphoreType.DMA((count, 3)),
            pltpu.SemaphoreType.DMA((count, 2)),
            pltpu.SemaphoreType.DMA((count, 2)),
            pltpu.SemaphoreType.DMA((count, 2)),
            pltpu.SemaphoreType.DMA((count, 2)),
        ],
        compiler_params=pltpu.CompilerParams(
            collective_id=0, has_side_effects=True, vmem_limit_bytes=32 * 1024 * 1024),
        cost_estimate=pl.CostEstimate(
            flops=4 * rows * rows * KV_STEPS * total_width,
            bytes_accessed=8 * rows * total_width,
            transcendentals=rows * rows * KV_STEPS * heads),
    )(*(pltpu.with_memory_space_constraint(x, pltpu.HBM) for x in (att_query, att_key, att_value)))
    return write(attn_out, attn_lse)


def solution(mesh):
    spec = P(("dp", "ctx"), None)
    return jax.shard_map(
        functools.partial(shards, mesh.shape["ctx"]),
        mesh=mesh,
        in_specs=(spec, spec, spec),
        out_specs=(spec, P(None, ("dp", "ctx"))),
        check_vma=False,
    )
```

```python
import functools
import math

import jax
import jax.numpy as jnp
from jax import lax
from jax.experimental import pallas as pl
from jax.experimental.pallas import tpu as pltpu
from jax.sharding import PartitionSpec as P

HEAD_DIM = 128
KV_STEPS = 3
CHUNK_HEADS = 2
AHEAD_ODD = 2
LAG = 1
MESH = pl.DeviceIdType.MESH


def kernel(
    n, q_hbm, k_hbm, v_hbm, o_ref, lse_ref,
    q_own, k_own, v_own, k_buf, v_buf, bias,
    in_sem, far_send, far_recv, near_send, near_recv,
):
    count, rows, width = k_own.shape
    chunk_heads = width // HEAD_DIM
    ahead = min(AHEAD_ODD, count)
    me = lax.axis_index("ctx")
    odd = lax.rem(me, 2) == 1
    even = jnp.logical_not(odd)
    partner = me + 1 - 2 * lax.rem(me, 2)
    has_far_target = me + 2 < n
    has_far_source = me >= 2
    has_near_source = me >= 1
    own = (k_own, v_own)
    bufs = (k_buf, v_buf)

    def columns(c):
        return pl.ds(pl.multiple_of(c * width, width), width)

    def far(c, t):
        return pltpu.make_async_remote_copy(
            src_ref=own[t].at[c], dst_ref=bufs[t].at[0, c],
            send_sem=far_send.at[c, t], recv_sem=far_recv.at[c, t],
            device_id={"ctx": lax.rem(me + 2, n)}, device_id_type=MESH)

    def near(c, t):
        return pltpu.make_async_remote_copy(
            src_ref=own[t].at[c], dst_ref=bufs[t].at[1, c],
            send_sem=near_send.at[c, t], recv_sem=near_recv.at[c, t],
            device_id={"ctx": partner}, device_id_type=MESH)

    def relay(c, t):
        return pltpu.make_async_remote_copy(
            src_ref=bufs[t].at[0, c], dst_ref=bufs[t].at[1, c],
            send_sem=near_send.at[c, t], recv_sem=near_recv.at[c, t],
            device_id={"ctx": partner}, device_id_type=MESH)

    def local(c, t):
        source = (k_hbm, v_hbm, q_hbm)[t]
        target = (k_own, v_own, q_own)[t]
        return pltpu.make_async_copy(source.at[:, columns(c)], target.at[c], in_sem.at[c, t])

    def each(start, stop, body):
        def step(c, carry):
            body(c)
            return carry
        lax.fori_loop(start, stop, step, 0)

    barrier = pltpu.get_barrier_semaphore()
    pl.semaphore_signal(barrier, inc=1, device_id={"ctx": partner}, device_id_type=MESH)

    @pl.when(has_far_target)
    def _():
        pl.semaphore_signal(barrier, inc=1, device_id={"ctx": lax.rem(me + 2, n)}, device_id_type=MESH)

    @pl.when(has_far_source)
    def _():
        pl.semaphore_signal(barrier, inc=1, device_id={"ctx": lax.rem(me + n - 2, n)}, device_id_type=MESH)

    def start_local(c):
        for t in range(2):
            local(c, t).start()

    each(0, count, start_local)

    pl.semaphore_wait(barrier, 1 + has_far_target.astype(jnp.int32) + has_far_source.astype(jnp.int32))

    def start_far(c):
        for t in range(2):
            far(c, t).start()

    def start_near(c):
        for t in range(2):
            near(c, t).start()

    def wait_local(c):
        for t in range(2):
            local(c, t).wait()

    def first_sends(c):
        wait_local(c)

        @pl.when(even)
        def _():
            start_near(c)

        @pl.when(has_far_target & (even | (c < ahead)))
        def _():
            start_far(c)

    each(0, count, first_sends)
    each(0, count, lambda c: local(c, 2).start())

    @pl.when(jnp.logical_not(has_far_source))
    def _():
        k_buf[0] = jnp.zeros(k_buf.shape[1:], k_buf.dtype)
        v_buf[0] = jnp.zeros(v_buf.shape[1:], v_buf.dtype)

    @pl.when(jnp.logical_not(has_near_source))
    def _():
        k_buf[1] = jnp.zeros(k_buf.shape[1:], k_buf.dtype)
        v_buf[1] = jnp.zeros(v_buf.shape[1:], v_buf.dtype)

    query = lax.broadcasted_iota(jnp.int32, (rows, KV_STEPS * rows), 0)
    key = lax.broadcasted_iota(jnp.int32, (rows, KV_STEPS * rows), 1)
    back = KV_STEPS - 1 - key // rows
    allowed = (back <= me) & ((back > 0) | (key - (KV_STEPS - 1) * rows <= query))
    bias[...] = jnp.where(allowed, 0.0, -jnp.inf)
    factor = math.log2(math.e) / math.sqrt(HEAD_DIM)

    each(0, count, lambda c: local(c, 2).wait())

    def scores(q, block, columns_of_bias):
        return lax.dot_general(
            q, block, (((1,), (1,)), ((), ())), preferred_element_type=jnp.float32
        ) + bias[:, columns_of_bias]

    far_place, near_place, own_place = (slice(i * rows, (i + 1) * rows) for i in range(KV_STEPS))

    def finish_chunk(c):
        @pl.when(even & has_far_source)
        def _():
            for t in range(2):
                far(c, t).wait_recv()

        places = [slice(h * HEAD_DIM, (h + 1) * HEAD_DIM) for h in range(chunk_heads)]
        first = []
        for place in places:
            q = q_own[c, :, place]
            s_far = scores(q, k_buf[0, c, :, place], far_place)
            s_own = scores(q, k_own[c, :, place], own_place)
            m = jnp.maximum(jnp.max(s_far, axis=1, keepdims=True), jnp.max(s_own, axis=1, keepdims=True))
            w_far = jnp.exp2((s_far - m) * factor)
            w_own = jnp.exp2((s_own - m) * factor)
            total = jnp.sum(w_far + w_own, axis=1, keepdims=True)
            mixed = jnp.dot(w_far.astype(jnp.bfloat16), v_buf[0, c, :, place], preferred_element_type=jnp.float32)
            mixed += jnp.dot(w_own.astype(jnp.bfloat16), v_own[c, :, place], preferred_element_type=jnp.float32)
            first.append((m, total, mixed))

        @pl.when(has_near_source)
        def _():
            near(c, 0).wait_recv()

        second = []
        for place, (m_first, total, mixed) in zip(places, first):
            s = scores(q_own[c, :, place], k_buf[1, c, :, place], near_place)
            m = jnp.maximum(m_first, jnp.max(s, axis=1, keepdims=True))
            w = jnp.exp2((s - m) * factor)
            scale = jnp.exp2((m_first - m) * factor)
            total = total * scale + jnp.sum(w, axis=1, keepdims=True)
            inverse = 1.0 / total
            second.append((w.astype(jnp.bfloat16), mixed * (scale * inverse), inverse))
            lse = m * (1.0 / math.sqrt(HEAD_DIM)) + jnp.log(total)
            diagonal = (lax.broadcasted_iota(jnp.int32, (rows, rows), 0)
                        == lax.broadcasted_iota(jnp.int32, (rows, rows), 1))
            lse_ref[pl.ds(c * chunk_heads + len(second) - 1, 1), :] = jnp.sum(
                jnp.where(diagonal, lse, 0.0), axis=0, keepdims=True)

        @pl.when(has_near_source)
        def _():
            near(c, 1).wait_recv()

        for h, (w, mixed, inverse) in enumerate(second):
            mixed += jnp.dot(w, v_buf[1, c, :, places[h]], preferred_element_type=jnp.float32) * inverse
            place = pl.ds(pl.multiple_of((c * chunk_heads + h) * HEAD_DIM, HEAD_DIM), HEAD_DIM)
            o_ref[:, place] = mixed.astype(o_ref.dtype)

    def wait_far_sends(c):
        for t in range(2):
            far(c, t).wait_send()

    def wait_near_sends(c):
        for t in range(2):
            near(c, t).wait_send()

    def step(c):
        @pl.when(odd & has_far_source & (c < count))
        def _():
            for t in range(2):
                far(c, t).wait_recv()
                relay(c, t).start()

        @pl.when(odd & has_far_target & (c + ahead < count))
        def _():
            start_far(c + ahead)

        @pl.when(c == count + LAG - 1)
        def _():
            @pl.when(has_far_target)
            def _():
                each(0, count, wait_far_sends)

            @pl.when(even | has_far_source)
            def _():
                each(0, count - 2, wait_near_sends)

        @pl.when(c >= LAG)
        def _():
            finish_chunk(c - LAG)

    each(0, count + LAG, step)

    @pl.when(even | has_far_source)
    def _():
        each(count - 2, count, wait_near_sends)


def write_kernel(o_vmem, lse_vmem, o_hbm, lse_hbm, sem):
    copies = [
        pltpu.make_async_copy(o_vmem, o_hbm, sem.at[0]),
        pltpu.make_async_copy(lse_vmem, lse_hbm, sem.at[1]),
    ]
    for copy in copies:
        copy.start()
    for copy in copies:
        copy.wait()


def write(attn_out, attn_lse):
    return pl.pallas_call(
        write_kernel,
        out_shape=(
            jax.ShapeDtypeStruct(attn_out.shape, attn_out.dtype),
            jax.ShapeDtypeStruct(attn_lse.shape, attn_lse.dtype),
        ),
        in_specs=[pl.BlockSpec(memory_space=pltpu.VMEM)] * 2,
        out_specs=(pl.BlockSpec(memory_space=pltpu.HBM),) * 2,
        scratch_shapes=[pltpu.SemaphoreType.DMA((2,))],
        compiler_params=pltpu.CompilerParams(vmem_limit_bytes=32 * 1024 * 1024),
        cost_estimate=pl.CostEstimate(
            flops=0, bytes_accessed=4 * attn_out.size, transcendentals=0),
    )(*(pltpu.with_memory_space_constraint(x, pltpu.VMEM) for x in (attn_out, attn_lse)))


def shards(n, att_query, att_key, att_value):
    rows, total_width = att_query.shape
    heads = total_width // HEAD_DIM
    chunk_heads = math.gcd(heads, CHUNK_HEADS)
    count = heads // chunk_heads
    width = chunk_heads * HEAD_DIM
    bf16 = att_query.dtype
    attn_out, attn_lse = pl.pallas_call(
        functools.partial(kernel, n),
        out_shape=(
            pltpu.VMEM((rows, total_width), bf16),
            pltpu.VMEM((heads, rows), jnp.float32),
        ),
        in_specs=[pl.BlockSpec(memory_space=pltpu.HBM)] * 3,
        out_specs=(pl.BlockSpec(memory_space=pltpu.VMEM), pl.BlockSpec(memory_space=pltpu.VMEM)),
        scratch_shapes=[
            pltpu.VMEM((count, rows, width), bf16),
            pltpu.VMEM((count, rows, width), bf16),
            pltpu.VMEM((count, rows, width), bf16),
            pltpu.VMEM((KV_STEPS - 1, count, rows, width), bf16),
            pltpu.VMEM((KV_STEPS - 1, count, rows, width), bf16),
            pltpu.VMEM((rows, KV_STEPS * rows), jnp.float32),
            pltpu.SemaphoreType.DMA((count, 3)),
            pltpu.SemaphoreType.DMA((count, 2)),
            pltpu.SemaphoreType.DMA((count, 2)),
            pltpu.SemaphoreType.DMA((count, 2)),
            pltpu.SemaphoreType.DMA((count, 2)),
        ],
        compiler_params=pltpu.CompilerParams(
            collective_id=0, has_side_effects=True, vmem_limit_bytes=32 * 1024 * 1024),
        cost_estimate=pl.CostEstimate(
            flops=4 * rows * rows * KV_STEPS * total_width,
            bytes_accessed=8 * rows * total_width,
            transcendentals=rows * rows * KV_STEPS * heads),
    )(*(pltpu.with_memory_space_constraint(x, pltpu.HBM) for x in (att_query, att_key, att_value)))
    return write(attn_out, attn_lse)


def solution(mesh):
    spec = P(("dp", "ctx"), None)
    return jax.shard_map(
        functools.partial(shards, mesh.shape["ctx"]),
        mesh=mesh,
        in_specs=(spec, spec, spec),
        out_specs=(spec, P(None, ("dp", "ctx"))),
        check_vma=False,
    )
```

```python
import functools
import math

import jax
import jax.numpy as jnp
from jax import lax
from jax.experimental import pallas as pl
from jax.experimental.pallas import tpu as pltpu
from jax.sharding import PartitionSpec as P

HEAD_DIM = 128
KV_STEPS = 3
CHUNK_HEADS = 2
AHEAD_ODD = 3
LAG = 1
MESH = pl.DeviceIdType.MESH


def kernel(
    n, q_hbm, k_hbm, v_hbm, o_ref, lse_ref,
    q_own, k_own, v_own, k_buf, v_buf, bias,
    in_sem, far_send, far_recv, near_send, near_recv,
):
    count, rows, width = k_own.shape
    chunk_heads = width // HEAD_DIM
    ahead = min(AHEAD_ODD, count)
    me = lax.axis_index("ctx")
    odd = lax.rem(me, 2) == 1
    even = jnp.logical_not(odd)
    partner = me + 1 - 2 * lax.rem(me, 2)
    has_far_target = me + 2 < n
    has_far_source = me >= 2
    has_near_source = me >= 1
    own = (k_own, v_own)
    bufs = (k_buf, v_buf)

    def columns(c):
        return pl.ds(pl.multiple_of(c * width, width), width)

    def far(c, t):
        return pltpu.make_async_remote_copy(
            src_ref=own[t].at[c], dst_ref=bufs[t].at[0, c],
            send_sem=far_send.at[c, t], recv_sem=far_recv.at[c, t],
            device_id={"ctx": lax.rem(me + 2, n)}, device_id_type=MESH)

    def near(c, t):
        return pltpu.make_async_remote_copy(
            src_ref=own[t].at[c], dst_ref=bufs[t].at[1, c],
            send_sem=near_send.at[c, t], recv_sem=near_recv.at[c, t],
            device_id={"ctx": partner}, device_id_type=MESH)

    def relay(c, t):
        return pltpu.make_async_remote_copy(
            src_ref=bufs[t].at[0, c], dst_ref=bufs[t].at[1, c],
            send_sem=near_send.at[c, t], recv_sem=near_recv.at[c, t],
            device_id={"ctx": partner}, device_id_type=MESH)

    def local(c, t):
        source = (k_hbm, v_hbm, q_hbm)[t]
        target = (k_own, v_own, q_own)[t]
        return pltpu.make_async_copy(source.at[:, columns(c)], target.at[c], in_sem.at[c, t])

    def each(start, stop, body):
        def step(c, carry):
            body(c)
            return carry
        lax.fori_loop(start, stop, step, 0)

    barrier = pltpu.get_barrier_semaphore()
    pl.semaphore_signal(barrier, inc=1, device_id={"ctx": partner}, device_id_type=MESH)

    @pl.when(has_far_target)
    def _():
        pl.semaphore_signal(barrier, inc=1, device_id={"ctx": lax.rem(me + 2, n)}, device_id_type=MESH)

    @pl.when(has_far_source)
    def _():
        pl.semaphore_signal(barrier, inc=1, device_id={"ctx": lax.rem(me + n - 2, n)}, device_id_type=MESH)

    def start_local(c):
        for t in range(3):
            local(c, t).start()

    each(0, count, start_local)

    pl.semaphore_wait(barrier, 1 + has_far_target.astype(jnp.int32) + has_far_source.astype(jnp.int32))

    def start_far(c):
        for t in range(2):
            far(c, t).start()

    def start_near(c):
        for t in range(2):
            near(c, t).start()

    def wait_local(c):
        for t in range(2):
            local(c, t).wait()

    def first_sends(c):
        wait_local(c)

        @pl.when(even)
        def _():
            start_near(c)

        @pl.when(has_far_target & (even | (c < ahead)))
        def _():
            start_far(c)

    each(0, count, first_sends)

    @pl.when(jnp.logical_not(has_far_source))
    def _():
        k_buf[0] = jnp.zeros(k_buf.shape[1:], k_buf.dtype)
        v_buf[0] = jnp.zeros(v_buf.shape[1:], v_buf.dtype)

    @pl.when(jnp.logical_not(has_near_source))
    def _():
        k_buf[1] = jnp.zeros(k_buf.shape[1:], k_buf.dtype)
        v_buf[1] = jnp.zeros(v_buf.shape[1:], v_buf.dtype)

    query = lax.broadcasted_iota(jnp.int32, (rows, KV_STEPS * rows), 0)
    key = lax.broadcasted_iota(jnp.int32, (rows, KV_STEPS * rows), 1)
    back = KV_STEPS - 1 - key // rows
    allowed = (back <= me) & ((back > 0) | (key - (KV_STEPS - 1) * rows <= query))
    bias[...] = jnp.where(allowed, 0.0, -jnp.inf)
    factor = math.log2(math.e) / math.sqrt(HEAD_DIM)

    def scores(q, block, columns_of_bias):
        return lax.dot_general(
            q, block, (((1,), (1,)), ((), ())), preferred_element_type=jnp.float32
        ) + bias[:, columns_of_bias]

    far_place, near_place, own_place = (slice(i * rows, (i + 1) * rows) for i in range(KV_STEPS))

    def finish_chunk(c):
        local(c, 2).wait()

        @pl.when(even & has_far_source)
        def _():
            for t in range(2):
                far(c, t).wait_recv()

        places = [slice(h * HEAD_DIM, (h + 1) * HEAD_DIM) for h in range(chunk_heads)]
        first = []
        for place in places:
            q = q_own[c, :, place]
            s_far = scores(q, k_buf[0, c, :, place], far_place)
            s_own = scores(q, k_own[c, :, place], own_place)
            m = jnp.maximum(jnp.max(s_far, axis=1, keepdims=True), jnp.max(s_own, axis=1, keepdims=True))
            w_far = jnp.exp2((s_far - m) * factor)
            w_own = jnp.exp2((s_own - m) * factor)
            total = jnp.sum(w_far + w_own, axis=1, keepdims=True)
            mixed = jnp.dot(w_far.astype(jnp.bfloat16), v_buf[0, c, :, place], preferred_element_type=jnp.float32)
            mixed += jnp.dot(w_own.astype(jnp.bfloat16), v_own[c, :, place], preferred_element_type=jnp.float32)
            first.append((m, total, mixed))

        @pl.when(has_near_source)
        def _():
            near(c, 0).wait_recv()

        second = []
        for place, (m_first, total, mixed) in zip(places, first):
            s = scores(q_own[c, :, place], k_buf[1, c, :, place], near_place)
            m = jnp.maximum(m_first, jnp.max(s, axis=1, keepdims=True))
            w = jnp.exp2((s - m) * factor)
            scale = jnp.exp2((m_first - m) * factor)
            total = total * scale + jnp.sum(w, axis=1, keepdims=True)
            inverse = 1.0 / total
            second.append((w.astype(jnp.bfloat16), mixed * (scale * inverse), inverse))
            lse = m * (1.0 / math.sqrt(HEAD_DIM)) + jnp.log(total)
            diagonal = (lax.broadcasted_iota(jnp.int32, (rows, rows), 0)
                        == lax.broadcasted_iota(jnp.int32, (rows, rows), 1))
            lse_ref[pl.ds(c * chunk_heads + len(second) - 1, 1), :] = jnp.sum(
                jnp.where(diagonal, lse, 0.0), axis=0, keepdims=True)

        @pl.when(has_near_source)
        def _():
            near(c, 1).wait_recv()

        for h, (w, mixed, inverse) in enumerate(second):
            mixed += jnp.dot(w, v_buf[1, c, :, places[h]], preferred_element_type=jnp.float32) * inverse
            place = pl.ds(pl.multiple_of((c * chunk_heads + h) * HEAD_DIM, HEAD_DIM), HEAD_DIM)
            o_ref[:, place] = mixed.astype(o_ref.dtype)

    def wait_far_sends(c):
        for t in range(2):
            far(c, t).wait_send()

    def wait_near_sends(c):
        for t in range(2):
            near(c, t).wait_send()

    def step(c):
        @pl.when(odd & has_far_source & (c < count))
        def _():
            for t in range(2):
                far(c, t).wait_recv()
                relay(c, t).start()

        @pl.when(odd & has_far_target & (c + ahead < count))
        def _():
            start_far(c + ahead)

        @pl.when(c == count + LAG - 1)
        def _():
            @pl.when(has_far_target)
            def _():
                each(0, count, wait_far_sends)

            @pl.when(even | has_far_source)
            def _():
                each(0, count - 2, wait_near_sends)

        @pl.when(c >= LAG)
        def _():
            finish_chunk(c - LAG)

    each(0, count + LAG, step)

    @pl.when(even | has_far_source)
    def _():
        each(count - 2, count, wait_near_sends)


def write_kernel(o_vmem, lse_vmem, o_hbm, lse_hbm, sem):
    copies = [
        pltpu.make_async_copy(o_vmem, o_hbm, sem.at[0]),
        pltpu.make_async_copy(lse_vmem, lse_hbm, sem.at[1]),
    ]
    for copy in copies:
        copy.start()
    for copy in copies:
        copy.wait()


def write(attn_out, attn_lse):
    return pl.pallas_call(
        write_kernel,
        out_shape=(
            jax.ShapeDtypeStruct(attn_out.shape, attn_out.dtype),
            jax.ShapeDtypeStruct(attn_lse.shape, attn_lse.dtype),
        ),
        in_specs=[pl.BlockSpec(memory_space=pltpu.VMEM)] * 2,
        out_specs=(pl.BlockSpec(memory_space=pltpu.HBM),) * 2,
        scratch_shapes=[pltpu.SemaphoreType.DMA((2,))],
        compiler_params=pltpu.CompilerParams(vmem_limit_bytes=32 * 1024 * 1024),
        cost_estimate=pl.CostEstimate(
            flops=0, bytes_accessed=4 * attn_out.size, transcendentals=0),
    )(*(pltpu.with_memory_space_constraint(x, pltpu.VMEM) for x in (attn_out, attn_lse)))


def shards(n, att_query, att_key, att_value):
    rows, total_width = att_query.shape
    heads = total_width // HEAD_DIM
    chunk_heads = math.gcd(heads, CHUNK_HEADS)
    count = heads // chunk_heads
    width = chunk_heads * HEAD_DIM
    bf16 = att_query.dtype
    attn_out, attn_lse = pl.pallas_call(
        functools.partial(kernel, n),
        out_shape=(
            pltpu.VMEM((rows, total_width), bf16),
            pltpu.VMEM((heads, rows), jnp.float32),
        ),
        in_specs=[pl.BlockSpec(memory_space=pltpu.HBM)] * 3,
        out_specs=(pl.BlockSpec(memory_space=pltpu.VMEM), pl.BlockSpec(memory_space=pltpu.VMEM)),
        scratch_shapes=[
            pltpu.VMEM((count, rows, width), bf16),
            pltpu.VMEM((count, rows, width), bf16),
            pltpu.VMEM((count, rows, width), bf16),
            pltpu.VMEM((KV_STEPS - 1, count, rows, width), bf16),
            pltpu.VMEM((KV_STEPS - 1, count, rows, width), bf16),
            pltpu.VMEM((rows, KV_STEPS * rows), jnp.float32),
            pltpu.SemaphoreType.DMA((count, 3)),
            pltpu.SemaphoreType.DMA((count, 2)),
            pltpu.SemaphoreType.DMA((count, 2)),
            pltpu.SemaphoreType.DMA((count, 2)),
            pltpu.SemaphoreType.DMA((count, 2)),
        ],
        compiler_params=pltpu.CompilerParams(
            collective_id=0, has_side_effects=True, vmem_limit_bytes=32 * 1024 * 1024),
        cost_estimate=pl.CostEstimate(
            flops=4 * rows * rows * KV_STEPS * total_width,
            bytes_accessed=8 * rows * total_width,
            transcendentals=rows * rows * KV_STEPS * heads),
    )(*(pltpu.with_memory_space_constraint(x, pltpu.HBM) for x in (att_query, att_key, att_value)))
    return write(attn_out, attn_lse)


def solution(mesh):
    spec = P(("dp", "ctx"), None)
    return jax.shard_map(
        functools.partial(shards, mesh.shape["ctx"]),
        mesh=mesh,
        in_specs=(spec, spec, spec),
        out_specs=(spec, P(None, ("dp", "ctx"))),
        check_vma=False,
    )
```
